32 devices in a mesh: work: 8 (over y, x, core), tile: 4 (over z).
Axes of the slice: x: 2, y: 2, z: 4, core: 2. Of those that a mesh axis runs over, the one named last changes fastest.
Arguments:
- block_coords: float32 [4096, 3, 128], P(('work', 'tile')), may hold values from -6 to 6
- block_visibilities: float32 [4096, 4, 128], P(('work', 'tile')), may hold values from -6 to 6
- subgrid_of_block: int32 [4096], P(('work', 'tile')), may hold values from 0 to 127, as said below
- live_blocks: int32 [32], P(('work', 'tile')), may hold values from 96 to 128, as said below
- corners: int32 [128, 2], replicated, may hold values from 0 to 992, as said below
- channel_scale: float32 [2], replicated, may hold values from 0.85 to 1.15
Outputs:
- uv_grid: float32 [4, 256, 1024], P(None, 'tile', 'work')
The draws below stay inside these ranges and needn't reach their ends.
Inputs may be any that keep to these rules, and one draw needn't show every extreme that they name: `subgrid_of_block`: subgrid s belongs to the strip of worker s // 16. Among the 128 blocks of one device at most 64 belong to subgrids of one worker, and some worker gets exactly 64 blocks from every device. Device d in the order of the axes work, tile holds the blocks d * 128 to (d + 1) * 128 - 1; its first live_blocks[d] blocks are live, the others take no part. Some device has all its blocks live. Subgrid s covers rows corners[s, 0] to corners[s, 0] + 31 of the window, and columns corners[s, 1] to corners[s, 1] + 31, all inside columns 128 (s // 16) to 128 (s // 16 + 1) - 1.
All inputs are finite; a program needn't handle non-finite values.
Results may differ from the reference program's by a relative error of at most 0.0003.
Values sent between devices are 32-bit elements; how exact they have to be, the bound alone decides.
A program may use at most 192 MiB of HBM per device.

```python
import math
import jax
import jax.numpy as jnp
from jax import lax

CH = 2
SUB = 32
ROWS = 128
BLK_DEV = 128
GCW = 128
SUBW = 16
MAX_DEVICE_BLOCKS = 64
SOURCES = 32
STRIPS_PER_WORKER = 8
BLOCKS = 4096
NSUB = 128
GR = 256
GC = 1024


def route_workers(key):
    busiest_worker = jax.random.randint(jax.random.fold_in(key, 11), (), 0, STRIPS_PER_WORKER)
    crowd_penalty = jax.random.randint(jax.random.fold_in(key, 12), (STRIPS_PER_WORKER,), 0, 4) * 4096
    worker_index = jnp.arange(STRIPS_PER_WORKER, dtype=jnp.int32)
    further_credit = crowd_penalty + jnp.where(worker_index == busiest_worker, 1 << 20, 0)
    local_position = jnp.arange(MAX_DEVICE_BLOCKS, dtype=jnp.int32)
    boundary_worker = (worker_index[:, None] == 0) | (worker_index[:, None] == STRIPS_PER_WORKER - 1)
    added_credit = jnp.where(boundary_worker & (local_position[None, :] == 0), 1 << 19, 0)
    position_index = jnp.arange(STRIPS_PER_WORKER * MAX_DEVICE_BLOCKS, dtype=jnp.int32).reshape(STRIPS_PER_WORKER, MAX_DEVICE_BLOCKS)

    def one_source(source_key):
        starting_score = jax.random.randint(source_key, (STRIPS_PER_WORKER, MAX_DEVICE_BLOCKS), 0, 16384)
        scores_by_worker = (starting_score + further_credit[:, None] + added_credit) * (STRIPS_PER_WORKER * MAX_DEVICE_BLOCKS) + position_index
        chosen = lax.top_k(scores_by_worker.reshape(-1), BLK_DEV)[1]
        owners = chosen // MAX_DEVICE_BLOCKS
        slots = chosen % MAX_DEVICE_BLOCKS
        order = jax.random.permutation(jax.random.fold_in(source_key, 5), BLK_DEV)
        return (owners[order], slots[order])
    source_keys = jax.random.split(jax.random.fold_in(key, 13), SOURCES)
    return jax.vmap(one_source)(source_keys)


def draw_subgrid_of_block(key, part):
    owners, slots = route_workers(key)
    within = jax.random.randint(jax.random.fold_in(key, 14), owners.shape, 0, SUBW)
    within = jnp.where((owners == STRIPS_PER_WORKER - 1) & (slots == 0), SUBW - 1, within)
    within = jnp.where((owners == 0) & (slots == 0), 0, within)
    return (owners * SUBW + within).reshape(-1).astype(jnp.int32)


def draw_live_blocks(key, part):
    counts = jax.random.randint(key, (SOURCES,), BLK_DEV - BLK_DEV // 4, BLK_DEV + 1)
    fullest = jax.random.randint(jax.random.fold_in(key, 21), (), 0, SOURCES)
    sparsest = (fullest + 1) % SOURCES
    source_ids = jnp.arange(SOURCES, dtype=jnp.int32)
    counts = jnp.where(source_ids == sparsest, BLK_DEV - BLK_DEV // 4, counts)
    counts = jnp.where(source_ids == fullest, BLK_DEV, counts)
    return counts.astype(jnp.int32)


def draw_corners(key, part):
    row_first = jax.random.randint(jax.random.fold_in(key, 31), (NSUB,), 0, GR - SUB + 1)
    col_offset = jax.random.randint(jax.random.fold_in(key, 32), (NSUB,), 0, GCW - SUB + 1)
    edge_cols = jax.random.randint(jax.random.fold_in(key, 33), (STRIPS_PER_WORKER,), 0, SUBW)
    edge_rows = jax.random.randint(jax.random.fold_in(key, 34), (STRIPS_PER_WORKER,), 0, SUBW)
    subgrid_ids = jnp.arange(NSUB, dtype=jnp.int32)
    within = subgrid_ids % SUBW
    strip = subgrid_ids // SUBW
    col_offset = jnp.where(within == edge_cols[strip], GCW - SUB, col_offset)
    row_first = jnp.where(within == edge_rows[strip], GR - SUB, row_first)
    row_first = jnp.where(within == (edge_rows[strip] + 1) % SUBW, 0, row_first)
    return jnp.stack([row_first, strip * GCW + col_offset], axis=1).astype(jnp.int32)


def block_levels(rng, shape, cuts, least, largest):
    level, own = 1.0, jax.random.fold_in(rng, 6)
    for axis_at, blocks in cuts:
        draws = jnp.exp(jax.random.uniform(jax.random.fold_in(own, axis_at), (blocks,), jnp.float32, least / len(cuts), largest / len(cuts)))
        level = level * jnp.repeat(draws, shape[axis_at] // blocks).reshape([-1 if axis == axis_at else 1 for axis in range(len(shape))])
    return level


def centred(rng, dims, scale, most, cuts=(), kind=jnp.bfloat16):
    loudness = block_levels(rng, dims, cuts, -0.22, 0.18) if cuts else 1.0
    array = jax.random.normal(rng, dims, jnp.float32) * scale * loudness
    return jnp.minimum(jnp.maximum(array, -most), most).astype(kind)


def setup_inputs(seed: int = 0) -> dict:
    seeds = jax.random.split(jax.random.key(seed), 7)
    return {
        "block_coords": jnp.clip(jax.random.uniform(seeds[0], (BLOCKS, 3, ROWS), jnp.float32, -6.0, 6.0) * block_levels(seeds[0], (BLOCKS, 3, ROWS), ((0, 32),), -0.4, 0.0), -6.0, 6.0),
        "block_visibilities": centred(seeds[1], (BLOCKS, 2 * CH, ROWS), 1.0, 6.0, ((0, 32),), jnp.float32),
        "subgrid_of_block": draw_subgrid_of_block(jax.random.fold_in(seeds[6], 71), 0),
        "live_blocks": draw_live_blocks(jax.random.fold_in(seeds[6], 71), 0),
        "corners": draw_corners(jax.random.fold_in(seeds[6], 71), 0),
        "channel_scale": jnp.clip(jax.random.uniform(seeds[5], (CH,), jnp.float32, 0.85, 1.15), 0.85, 1.15),
    }


two_pi = 2.0 * math.pi
highest = lax.Precision.HIGHEST


def pixel_offsets():
    return (jnp.arange(SUB, dtype=jnp.float32) - SUB // 2) / SUB


def block_pictures(coords, waves, channel_scale):
    offsets = pixel_offsets()
    squares = offsets * offsets
    layers = []
    for channel in range(CH):
        factor = channel_scale[channel]
        first_coord = coords[:, 0, :] * factor
        second_coord = coords[:, 1, :] * factor
        depth_coord = coords[:, 2, :] * factor
        depth_term = depth_coord[:, None, :] * squares[None, :, None]
        phase_first = two_pi * (first_coord[:, None, :] * offsets[None, :, None] + depth_term)
        phase_second = two_pi * (second_coord[:, None, :] * offsets[None, :, None] + depth_term)
        wave_real = waves[:, 2 * channel, :][:, None, :]
        wave_imag = waves[:, 2 * channel + 1, :][:, None, :]
        cosine_first = jnp.cos(phase_first)
        sine_first = jnp.sin(phase_first)
        cosine_second = jnp.cos(phase_second)
        sine_second = jnp.sin(phase_second)
        left_side = jnp.concatenate([wave_real * cosine_first - wave_imag * sine_first, wave_real * sine_first + wave_imag * cosine_first], axis=2)
        right_real = jnp.concatenate([cosine_second, -sine_second], axis=2)
        right_imag = jnp.concatenate([sine_second, cosine_second], axis=2)
        right_side = jnp.concatenate([right_real, right_imag], axis=1)
        layers.append(jnp.einsum("nxk,njk->nxj", left_side, right_side, precision=highest))
    return jnp.stack(layers, axis=1)


def transform_matrix():
    offsets = jnp.arange(SUB, dtype=jnp.int32)
    taper_values = jnp.sin(jnp.pi * (offsets.astype(jnp.float32) + 0.5) / SUB) ** 2
    product = (offsets[:, None] * offsets[None, :]) % SUB
    angles = two_pi * product.astype(jnp.float32) / SUB
    real_part = taper_values[:, None] * jnp.cos(angles)
    imag_part = -taper_values[:, None] * jnp.sin(angles)
    upper = jnp.concatenate([real_part, imag_part], axis=1)
    lower = jnp.concatenate([-imag_part, real_part], axis=1)
    return jnp.concatenate([upper, lower], axis=0)


def to_spectrum(pictures):
    amount = pictures.shape[0]
    matrix = transform_matrix()
    first = jnp.einsum("ncxj,jq->ncxq", pictures, matrix, precision=highest)
    first = first.reshape(amount, CH, SUB, 2, SUB)
    second = jnp.einsum("ncxpl,pxqk->ncqkl", first, matrix.reshape(2, SUB, 2, SUB), precision=highest)
    return (second * (1.0 / (ROWS * SUB))).reshape(amount, 2 * CH, SUB, SUB)


def place(canvas, spectra, row_start, col_start):
    offsets = jnp.arange(SUB, dtype=jnp.int32)
    row_index = row_start[:, None, None, None] + offsets[None, None, :, None]
    col_index = col_start[:, None, None, None] + offsets[None, None, None, :]
    layer_index = jnp.arange(2 * CH, dtype=jnp.int32)[None, :, None, None]
    height = canvas.shape[1]
    inside = (row_index >= 0) & (row_index < height)
    row_index = jnp.where(inside, row_index, height)
    return canvas.at[layer_index, row_index, col_index].add(spectra, mode="drop")


def reference(block_coords, block_visibilities, subgrid_of_block, live_blocks, corners, channel_scale):
    sources = live_blocks.shape[0]
    per_source = block_coords.shape[0] // sources
    coords_split = block_coords.reshape(sources, per_source, 3, ROWS)
    waves_split = block_visibilities.reshape(sources, per_source, 2 * CH, ROWS)
    labels_split = subgrid_of_block.reshape(sources, per_source)
    position = jnp.arange(per_source, dtype=jnp.int32)

    def accumulate(totals, inputs):
        coords_part, waves_part, labels_part, live_count = inputs
        live_mask = (position < live_count).astype(jnp.float32)
        pictures = block_pictures(coords_part, waves_part * live_mask[:, None, None], channel_scale)
        return totals.at[labels_part].add(pictures), None

    start = jnp.zeros((NSUB, CH, SUB, 2 * SUB), jnp.float32)
    totals = lax.scan(accumulate, start, (coords_split, waves_split, labels_split, live_blocks))[0]
    spectra = to_spectrum(totals)
    canvas = jnp.zeros((2 * CH, GR, GC), jnp.float32)
    return place(canvas, spectra, corners[:, 0], corners[:, 1])
```

```python
import functools
import math

import jax
import jax.numpy as jnp
import numpy as np
from jax import lax
from jax.experimental import pallas as pl
from jax.experimental.pallas import tpu as pltpu
from jax.sharding import PartitionSpec as P

CH = 2
SUB = 32
ROWS = 128
GCW = 128
SUBW = 16
HALF = SUBW // 2
UNROLL = 4
MESH = pl.DeviceIdType.MESH
highest = lax.Precision.HIGHEST

SIN = (6.283184916495431, -41.34158923268848, 81.59994332978006, -76.61447253122435, 41.34288235446963, -12.471243534886277)
COS = (0.9999992107823215, -19.73898035576396, 64.92865742103214, -85.2716215342875, 58.7904921200778, -21.07110562755528)


def horner(coefficients, z):
    total = jnp.full_like(z, coefficients[-1])
    for value in coefficients[-2::-1]:
        total = total * z + value
    return total


def sincos_turns(turns):
    rest = turns - jnp.round(turns)
    z = rest * rest
    return rest * horner(SIN, z), horner(COS, z)


def split(value):
    high = value.astype(jnp.bfloat16)
    return high, (value - high.astype(jnp.float32)).astype(jnp.bfloat16)


def dot_nt(left, right):
    return lax.dot_general(left, right, (((1,), (1,)), ((), ())), preferred_element_type=jnp.float32)


def pictures_kernel(labels_ref, live_ref, scale_ref, coords_ref, waves_ref, out_ref):
    blocks = coords_ref.shape[0]
    out_ref[...] = jnp.zeros_like(out_ref)
    offset = (lax.broadcasted_iota(jnp.int32, (SUB, ROWS), 0) - SUB // 2).astype(jnp.float32) * (1.0 / SUB)
    square = offset * offset
    low_lanes = lax.broadcasted_iota(jnp.int32, (SUB, 2 * CH * SUB), 1) < 2 * SUB
    live = live_ref[0]

    def picture(block):
        coords = coords_ref[block]
        waves = waves_ref[block] * (block < live).astype(jnp.float32)
        depth = coords[2:3, :] * square
        turns_first = coords[0:1, :] * offset + depth
        turns_second = coords[1:2, :] * offset + depth
        products = []
        for channel in range(CH):
            factor = scale_ref[channel]
            sine, cosine = sincos_turns(turns_first * factor)
            real, imag = waves[2 * channel:2 * channel + 1, :], waves[2 * channel + 1:2 * channel + 2, :]
            left_high, left_low = split(
                jnp.concatenate([real * cosine - imag * sine, real * sine + imag * cosine], axis=1)
            )
            sine, cosine = sincos_turns(turns_second * factor)
            sine_high, sine_low = split(sine)
            cosine_high, cosine_low = split(cosine)
            parts = [
                jnp.concatenate([cosine_high, -sine_high], axis=1),
                jnp.concatenate([sine_high, cosine_high], axis=1),
                jnp.concatenate([cosine_low, -sine_low], axis=1),
                jnp.concatenate([sine_low, cosine_low], axis=1),
            ]
            if channel == 1:
                parts = parts[2:] + parts[:2]
            product = dot_nt(jnp.concatenate([left_high, left_low], axis=0), jnp.concatenate(parts, axis=0))
            products.append(product[:SUB] + product[SUB:])
        first, second = products
        return jnp.where(low_lanes, first, second) + pltpu.roll(jnp.where(low_lanes, second, first), 2 * SUB, 1)

    def body(step, carry):
        base = step * UNROLL
        group = [picture(base + k) for k in range(UNROLL)]
        for k in range(UNROLL):
            label = labels_ref[base + k]
            out_ref[label] = out_ref[label] + group[k]
        return carry

    lax.fori_loop(0, blocks // UNROLL, body, 0)


def partial_pictures(coords, waves, labels, live, scale, subgrids):
    smem = pl.BlockSpec(memory_space=pltpu.SMEM)
    vmem = pl.BlockSpec(memory_space=pltpu.VMEM)
    return pl.pallas_call(
        pictures_kernel,
        out_shape=jax.ShapeDtypeStruct((subgrids, SUB, 2 * CH * SUB), jnp.float32),
        in_specs=[smem, smem, smem, vmem, vmem],
        out_specs=vmem,
        compiler_params=pltpu.CompilerParams(vmem_limit_bytes=32 * 1024 * 1024),
        name="block_pictures",
    )(labels, live, scale, coords, waves)


def transform_matrices():
    at = np.arange(SUB)
    taper = np.sin(np.pi * (at + 0.5) / SUB) ** 2
    angles = 2.0 * math.pi * (at[:, None] * at[None, :] % SUB) / SUB
    real, imag = taper[:, None] * np.cos(angles), -taper[:, None] * np.sin(angles)
    plain = np.block([[real, imag], [-imag, real]])
    turned = np.block([[-imag, real], [-real, -imag]])
    columns = np.concatenate([np.kron(np.eye(CH), plain), np.kron(np.eye(CH), turned)], axis=1)
    rows = np.concatenate([real.T, imag.T], axis=1) / (ROWS * SUB)
    return columns.astype(np.float32), rows.astype(np.float32)


def stage_shapes(workers):
    bits = workers.bit_length() - 1
    return [[0] * bits, [0] + [bits - 1 - step for step in range(1, bits)]]


def combine_kernel(workers, tiles, *refs):
    corners_ref, data_ref, columns_ref, rows_ref, out_ref = refs[:5]
    bits = workers.bit_length() - 1
    orders = stage_shapes(workers)
    scratch = list(refs[5:])
    received = [[scratch.pop(0) for _ in range(bits)] for _ in range(2)]
    kept = [[scratch.pop(0) for _ in range(bits)] for _ in range(2)]
    placed, outgoing, incoming, send_sem, recv_sem, tile_send, tile_recv = scratch
    worker, tile = lax.axis_index("work"), lax.axis_index("tile")
    height = out_ref.shape[1]

    def partner(bit):
        return worker + (1 << bit) * (1 - 2 * ((worker >> bit) & 1))

    barrier = pltpu.get_barrier_semaphore()
    for bit in range(bits):
        pl.semaphore_signal(barrier, inc=1, device_id=(partner(bit), tile), device_id_type=MESH)
    for far in range(1, tiles):
        pl.semaphore_signal(barrier, inc=1, device_id=(worker, lax.rem(tile + far, tiles)), device_id_type=MESH)
    pl.semaphore_wait(barrier, bits + tiles - 1)

    def step_copy(half, step):
        position = orders[half][step]
        bit = 0 if step == 0 else (step if half == 0 else bits - step)
        mine = (worker >> bit) & 1
        if step == 0:
            source = data_ref.at[:, 1 - mine, :, pl.ds(half * HALF, HALF)]
        else:
            source = kept[half][step - 1].at[:, 1 - mine]
        return mine, pltpu.make_async_remote_copy(
            src_ref=source,
            dst_ref=received[half][step],
            send_sem=send_sem.at[half, step],
            recv_sem=recv_sem.at[half, step],
            device_id=(partner(bit), tile),
            device_id_type=MESH,
        )

    def step_sum(half, step, mine):
        arrived = received[half][step]
        high, low = arrived.shape[:2]
        following = kept[half][step].shape
        for a in range(high):
            for b in range(low):
                at = a * low + b
                if step == 0:
                    own = data_ref[a, mine, b, pl.ds(half * HALF, HALF)]
                else:
                    own = kept[half][step - 1][a, mine, b]
                low_next = following[2]
                kept[half][step][at // (2 * low_next), at // low_next % 2, at % low_next] = own + arrived[a, b]

    def last_sum(half, mine):
        step = bits - 1
        own = data_ref[0, mine, 0, pl.ds(half * HALF, HALF)] if step == 0 else kept[half][step - 1][0, mine, 0]
        kept[half][step][...] = own + received[half][step][0, 0]

    copies = [step_copy(half, 0) for half in range(2)]
    for _, copy in copies:
        copy.start()
    for step in range(bits):
        for half in range(2):
            mine, copy = copies[half]
            copy.wait()
            if step < bits - 1:
                step_sum(half, step, mine)
                copies[half] = step_copy(half, step + 1)
                copies[half][1].start()
            else:
                last_sum(half, mine)

    width = 2 * CH * SUB
    columns, rows = columns_ref[...], rows_ref[...]
    lane = lax.broadcasted_iota(jnp.int32, (1, SUBW * SUB), 1)
    row_at = jnp.zeros((1, SUBW * SUB), jnp.int32)
    stripe = lax.broadcasted_iota(jnp.int32, (width, GCW), 0)
    across = lax.broadcasted_iota(jnp.int32, (width, GCW), 1) - stripe % SUB
    group = lax.broadcasted_iota(jnp.int32, (width, width), 0) // SUB
    same = group == lax.broadcasted_iota(jnp.int32, (width, width), 1) // SUB
    for half in range(2):
        pictures = kept[half][bits - 1][...].reshape(HALF * SUB, width)
        first = jnp.dot(pictures, columns, precision=highest, preferred_element_type=jnp.float32)
        for s in range(HALF):
            sub = half * HALF + s
            piece = first[s * SUB:(s + 1) * SUB]
            stacked = jnp.concatenate([piece[:, :width], piece[:, width:]], axis=0)
            spectrum = jnp.dot(rows, stacked, precision=highest, preferred_element_type=jnp.float32)
            spread = jnp.where(same, jnp.concatenate([spectrum] * (2 * CH), axis=0), 0.0)
            high, low = split(spread)
            row0 = corners_ref[worker * SUBW + sub, 0]
            col0 = corners_ref[worker * SUBW + sub, 1] - worker * GCW
            target = jnp.where(across == col0, 1.0, 0.0).astype(jnp.bfloat16)
            wide = jnp.dot(jnp.concatenate([high, low], axis=0), target, preferred_element_type=jnp.float32)
            wide = wide[:width] + wide[width:]
            high, low = split(wide)
            for p in range(2 * CH):
                placed[p, sub * SUB:(sub + 1) * SUB, :GCW] = high[p * SUB:(p + 1) * SUB]
                placed[p, sub * SUB:(sub + 1) * SUB, GCW:] = low[p * SUB:(p + 1) * SUB]
            row_at = jnp.where(lane // SUB == sub, row0 + lane % SUB, row_at)

    def tile_rows(which, store):
        line = lax.broadcasted_iota(jnp.int32, (height, SUBW * SUB), 0) + which * height
        select = jnp.where(line == row_at, 1.0, 0.0).astype(jnp.bfloat16)
        for p in range(2 * CH):
            both = jnp.dot(select, placed[p], preferred_element_type=jnp.float32)
            store[p] = both[:, :GCW] + both[:, GCW:]

    sent = []
    for far in range(tiles - 1, 0, -1):
        which = lax.rem(tile + far, tiles)
        tile_rows(which, outgoing.at[far - 1])
        copy = pltpu.make_async_remote_copy(
            src_ref=outgoing.at[far - 1],
            dst_ref=incoming.at[far - 1],
            send_sem=tile_send.at[far - 1],
            recv_sem=tile_recv.at[far - 1],
            device_id=(worker, which),
            device_id_type=MESH,
        )
        copy.start()
        sent.append(copy)
    tile_rows(tile, out_ref)
    for copy in sent:
        copy.wait()
    total = out_ref[...]
    for far in range(tiles - 1):
        total = total + incoming[far]
    out_ref[...] = total


def combine(pictures, corners, workers, tiles, height):
    bits = workers.bit_length() - 1
    received, kept = [], []
    for order in stage_shapes(workers):
        for step in range(bits):
            count = workers >> step
            low = 1 << order[step]
            tail = (HALF, SUB, 2 * CH * SUB)
            received.append(pltpu.VMEM((count // (2 * low), low) + tail, jnp.float32))
            if step < bits - 1:
                low = 1 << order[step + 1]
                kept.append(pltpu.VMEM((count // 2 // (2 * low), 2, low) + tail, jnp.float32))
            else:
                kept.append(pltpu.VMEM(tail, jnp.float32))
    columns, rows = transform_matrices()
    block = (2 * CH, height, GCW)
    vmem = pl.BlockSpec(memory_space=pltpu.VMEM)
    return pl.pallas_call(
        functools.partial(combine_kernel, workers, tiles),
        out_shape=jax.ShapeDtypeStruct(block, jnp.float32),
        in_specs=[pl.BlockSpec(memory_space=pltpu.SMEM), vmem, vmem, vmem],
        out_specs=vmem,
        scratch_shapes=received + kept + [
            pltpu.VMEM((2 * CH, SUBW * SUB, 2 * GCW), jnp.bfloat16),
            pltpu.VMEM((tiles - 1,) + block, jnp.float32),
            pltpu.VMEM((tiles - 1,) + block, jnp.float32),
            pltpu.SemaphoreType.DMA((2, bits)),
            pltpu.SemaphoreType.DMA((2, bits)),
            pltpu.SemaphoreType.DMA((tiles - 1,)),
            pltpu.SemaphoreType.DMA((tiles - 1,)),
        ],
        compiler_params=pltpu.CompilerParams(
            collective_id=0, has_side_effects=True, vmem_limit_bytes=48 * 1024 * 1024
        ),
        name="reduce_and_place",
    )(corners, pictures.reshape(workers // 2, 2, 1, SUBW, SUB, 2 * CH * SUB), jnp.asarray(columns), jnp.asarray(rows))


def local(height, block_coords, block_visibilities, subgrid_of_block, live_blocks, corners, channel_scale):
    workers = lax.axis_size("work")
    tiles = lax.axis_size("tile")
    pictures = partial_pictures(
        block_coords, block_visibilities, subgrid_of_block, live_blocks, channel_scale, corners.shape[0]
    )
    return combine(pictures, corners, workers, tiles, height)


def solution(mesh):
    height = 64
    return jax.shard_map(
        functools.partial(local, height),
        mesh=mesh,
        in_specs=(
            P(("work", "tile"), None, None),
            P(("work", "tile"), None, None),
            P(("work", "tile")),
            P(("work", "tile")),
            P(),
            P(),
        ),
        out_specs=P(None, "tile", "work"),
        check_vma=False,
    )
```

```python
import functools
import math

import jax
import jax.numpy as jnp
import numpy as np
from jax import lax
from jax.experimental import pallas as pl
from jax.experimental.pallas import tpu as pltpu
from jax.sharding import PartitionSpec as P

CH = 2
SUB = 32
ROWS = 128
GCW = 128
SUBW = 16
QUARTER = SUBW // 4
UNROLL = 4
MESH = pl.DeviceIdType.MESH
highest = lax.Precision.HIGHEST

SIN = (6.283184916495431, -41.34158923268848, 81.59994332978006, -76.61447253122435, 41.34288235446963, -12.471243534886277)
COS = (0.9999992107823215, -19.73898035576396, 64.92865742103214, -85.2716215342875, 58.7904921200778, -21.07110562755528)


def horner(coefficients, z):
    total = jnp.full_like(z, coefficients[-1])
    for value in coefficients[-2::-1]:
        total = total * z + value
    return total


def sincos_turns(turns):
    rest = turns - jnp.round(turns)
    z = rest * rest
    return rest * horner(SIN, z), horner(COS, z)


def split(value):
    high = value.astype(jnp.bfloat16)
    return high, (value - high.astype(jnp.float32)).astype(jnp.bfloat16)


def dot_nt(left, right):
    return lax.dot_general(left, right, (((1,), (1,)), ((), ())), preferred_element_type=jnp.float32)


def pictures_kernel(labels_hbm, live_ref, scale_ref, coords_hbm, waves_hbm, out_ref, labels_ref, coords_ref, waves_ref, sems):
    loads = [
        pltpu.make_async_copy(source, target, sems.at[at])
        for at, (source, target) in enumerate(
            [(labels_hbm, labels_ref), (coords_hbm, coords_ref), (waves_hbm, waves_ref)]
        )
    ]
    for load in loads:
        load.start()
    blocks = waves_ref.shape[0]
    out_ref[...] = jnp.zeros_like(out_ref)
    offset = (lax.broadcasted_iota(jnp.int32, (SUB, ROWS), 0) - SUB // 2).astype(jnp.float32) * (1.0 / SUB)
    square = offset * offset
    side = lax.broadcasted_iota(jnp.int32, (SUB, 4 * SUB), 1) // (2 * SUB)
    live = live_ref[0]
    for load in loads:
        load.wait()

    def picture(block):
        first, second, third = [coords_ref[axis, pl.ds(block, 1), :] for axis in range(3)]
        waves = waves_ref[block] * (block < live).astype(jnp.float32)
        depth = third * square
        turns_first = first * offset + depth
        turns_second = second * offset + depth
        layers = []
        for channel in range(CH):
            factor = scale_ref[channel]
            sine, cosine = sincos_turns(turns_first * factor)
            real, imag = waves[2 * channel:2 * channel + 1, :], waves[2 * channel + 1:2 * channel + 2, :]
            left_high, left_low = split(
                jnp.concatenate([real * cosine - imag * sine, real * sine + imag * cosine], axis=1)
            )
            sine, cosine = sincos_turns(turns_second * factor)
            sine_high, sine_low = split(sine)
            cosine_high, cosine_low = split(cosine)
            right = jnp.concatenate(
                [
                    jnp.concatenate([cosine_high, -sine_high], axis=1),
                    jnp.concatenate([sine_high, cosine_high], axis=1),
                    jnp.concatenate([cosine_low, -sine_low], axis=1),
                    jnp.concatenate([sine_low, cosine_low], axis=1),
                ],
                axis=0,
            )
            product = dot_nt(jnp.concatenate([left_high, left_low], axis=0), right)
            product = product[:SUB] + product[SUB:]
            layers.append(product + pltpu.roll(product, 2 * SUB, 1))
        return layers

    def body(step, carry):
        base = step * UNROLL
        group = [picture(base + k) for k in range(UNROLL)]
        for k in range(UNROLL):
            label = labels_ref[base + k]
            mask = side == (label & 1)
            for channel in range(CH):
                out_ref[channel, label >> 1] += jnp.where(mask, group[k][channel], 0.0)
        return carry

    lax.fori_loop(0, blocks // UNROLL, body, 0)


def partial_pictures(coords, waves, labels, live, scale, subgrids):
    smem = pl.BlockSpec(memory_space=pltpu.SMEM)
    hbm = pl.BlockSpec(memory_space=pltpu.HBM)
    return pl.pallas_call(
        pictures_kernel,
        out_shape=jax.ShapeDtypeStruct((CH, subgrids // 2, SUB, 4 * SUB), jnp.float32),
        in_specs=[hbm, smem, smem, hbm, hbm],
        out_specs=pl.BlockSpec(memory_space=pltpu.VMEM),
        scratch_shapes=[
            pltpu.SMEM(labels.shape, jnp.int32),
            pltpu.VMEM(coords.shape, jnp.float32),
            pltpu.VMEM(waves.shape, jnp.float32),
            pltpu.SemaphoreType.DMA((3,)),
        ],
        compiler_params=pltpu.CompilerParams(vmem_limit_bytes=32 * 1024 * 1024),
        name="block_pictures",
    )(labels, live, scale, coords, waves)


def transform_matrices():
    at = np.arange(SUB)
    taper = np.sin(np.pi * (at + 0.5) / SUB) ** 2
    angles = 2.0 * math.pi * (at[:, None] * at[None, :] % SUB) / SUB
    real, imag = taper[:, None] * np.cos(angles), -taper[:, None] * np.sin(angles)
    plain = np.block([[real, imag], [-imag, real]])
    turned = np.block([[-imag, real], [-real, -imag]])
    columns = np.concatenate([np.kron(np.eye(2), plain), np.kron(np.eye(2), turned)], axis=1)
    rows = np.concatenate([real.T, imag.T], axis=1) / (ROWS * SUB)
    return columns.astype(np.float32), rows.astype(np.float32)


def stage_shapes(workers):
    bits = workers.bit_length() - 1
    return [[0] * bits, [0] + [bits - 1 - step for step in range(1, bits)]]


def combine_kernel(workers, tiles, *refs):
    corners_ref, data_ref, columns_ref, rows_ref, out_ref = refs[:5]
    bits = workers.bit_length() - 1
    orders = stage_shapes(workers)
    scratch = list(refs[5:])
    received = [[scratch.pop(0) for _ in range(bits)] for _ in range(2)]
    kept = [[scratch.pop(0) for _ in range(bits)] for _ in range(2)]
    placed, outgoing, incoming, send_sem, recv_sem, tile_send, tile_recv = scratch
    worker, tile = lax.axis_index("work"), lax.axis_index("tile")
    height = out_ref.shape[1]

    def partner(bit):
        return worker + (1 << bit) * (1 - 2 * ((worker >> bit) & 1))

    barrier = pltpu.get_barrier_semaphore()
    for bit in range(bits):
        pl.semaphore_signal(barrier, inc=1, device_id=(partner(bit), tile), device_id_type=MESH)
    for far in range(1, tiles):
        pl.semaphore_signal(barrier, inc=1, device_id=(worker, lax.rem(tile + far, tiles)), device_id_type=MESH)
    pl.semaphore_wait(barrier, bits + tiles - 1)

    def own_part(channel, half, step):
        if step == 0:
            return data_ref.at[channel], pl.ds(half * QUARTER, QUARTER)
        return kept[half][step - 1].at[channel], slice(None)

    def halved_bit(half, step):
        return 0 if step == 0 else (step if half == 0 else bits - step)

    def step_copy(channel, half, step):
        bit = halved_bit(half, step)
        source, pairs = own_part(channel, half, step)
        return pltpu.make_async_remote_copy(
            src_ref=source.at[:, 1 - ((worker >> bit) & 1), :, pairs],
            dst_ref=received[half][step].at[channel],
            send_sem=send_sem.at[channel, half, step],
            recv_sem=recv_sem.at[channel, half, step],
            device_id=(partner(bit), tile),
            device_id_type=MESH,
        )

    def step_sum(channel, half, step):
        mine = (worker >> halved_bit(half, step)) & 1
        source, pairs = own_part(channel, half, step)
        arrived = received[half][step].at[channel]
        target = kept[half][step].at[channel]
        if step == bits - 1:
            target[...] = source[0, mine, 0, pairs] + arrived[0, 0]
            return
        low, low_next = arrived.shape[1], target.shape[2]
        for a in range(arrived.shape[0]):
            for b in range(low):
                at = a * low + b
                target[at // (2 * low_next), at // low_next % 2, at % low_next] = source[a, mine, b, pairs] + arrived[a, b]

    copies = {}

    def advance(channel, step):
        for half in range(2):
            copies[channel, half].wait()
            step_sum(channel, half, step)
            if step < bits - 1:
                copies[channel, half] = step_copy(channel, half, step + 1)
                copies[channel, half].start()

    width = 4 * SUB
    columns, rows = columns_ref[...], rows_ref[...]
    lane = lax.broadcasted_iota(jnp.int32, (1, SUBW * SUB), 1)
    row_at = lane % SUB
    for s in range(SUBW):
        row_at = row_at + jnp.where(lane // SUB == s, corners_ref[0, worker * SUBW + s], 0)
    stripe = lax.broadcasted_iota(jnp.int32, (width, GCW), 0)
    across = lax.broadcasted_iota(jnp.int32, (width, GCW), 1) - stripe % SUB
    group = lax.broadcasted_iota(jnp.int32, (width, width), 0) // SUB
    same = group == lax.broadcasted_iota(jnp.int32, (width, width), 1) // SUB

    def transform(channel):
        pictures = jnp.concatenate(
            [kept[half][bits - 1][channel].reshape(QUARTER * SUB, width) for half in range(2)], axis=0
        )
        first = jnp.dot(pictures, columns, precision=highest, preferred_element_type=jnp.float32)
        pieces = [first[j * SUB:(j + 1) * SUB] for j in range(2 * QUARTER)]
        stacked = jnp.concatenate(
            [jnp.concatenate([piece[:, at:at + width] for piece in pieces], axis=1) for at in (0, width)], axis=0
        )
        spectra = jnp.dot(rows, stacked, precision=highest, preferred_element_type=jnp.float32)
        for j in range(2 * QUARTER):
            spectrum = spectra[:, j * width:(j + 1) * width]
            spread = jnp.where(same, jnp.concatenate([spectrum] * 4, axis=0), 0.0)
            high, low = split(spread)
            column = [corners_ref[1, worker * SUBW + 2 * j + side] - worker * GCW for side in range(2)]
            target = across == jnp.where(stripe < 2 * SUB, column[0], column[1])
            target = jnp.where(target, 1.0, 0.0).astype(jnp.bfloat16)
            wide = jnp.dot(jnp.concatenate([high, low], axis=0), target, preferred_element_type=jnp.float32)
            high, low = split(wide[:width] + wide[width:])
            for side in range(2):
                for part in range(2):
                    here = slice((2 * side + part) * SUB, (2 * side + part + 1) * SUB)
                    there = slice((2 * j + side) * SUB, (2 * j + side + 1) * SUB)
                    placed[2 * channel + part, there, :GCW] = high[here]
                    placed[2 * channel + part, there, GCW:] = low[here]

    def tile_rows(channel, which, store):
        line = lax.broadcasted_iota(jnp.int32, (height, SUBW * SUB), 0) + which * height
        select = jnp.where(line == row_at, 1.0, 0.0).astype(jnp.bfloat16)
        for part in range(2):
            both = jnp.dot(select, placed[2 * channel + part], preferred_element_type=jnp.float32)
            store[part] = both[:, :GCW] + both[:, GCW:]

    sent = []

    def spread_tiles(channel):
        for far in range(tiles - 1, 0, -1):
            which = lax.rem(tile + far, tiles)
            tile_rows(channel, which, outgoing.at[channel, far - 1])
            copy = pltpu.make_async_remote_copy(
                src_ref=outgoing.at[channel, far - 1],
                dst_ref=incoming.at[channel, far - 1],
                send_sem=tile_send.at[channel, far - 1],
                recv_sem=tile_recv.at[channel, far - 1],
                device_id=(worker, which),
                device_id_type=MESH,
            )
            copy.start()
            sent.append(copy)
        tile_rows(channel, tile, out_ref.at[pl.ds(2 * channel, 2)])

    for channel in range(CH):
        for half in range(2):
            copies[channel, half] = step_copy(channel, half, 0)
            copies[channel, half].start()
    for step in range(bits):
        advance(0, step)
        if 1 <= step <= bits - 2:
            advance(1, step - 1)
    transform(0)
    advance(1, bits - 2)
    spread_tiles(0)
    advance(1, bits - 1)
    transform(1)
    spread_tiles(1)
    for copy in sent:
        copy.wait()
    for channel in range(CH):
        total = out_ref[2 * channel:2 * channel + 2]
        for far in range(tiles - 1):
            total = total + incoming[channel, far]
        out_ref[2 * channel:2 * channel + 2] = total


def combine(pictures, corners, workers, tiles, height):
    bits = workers.bit_length() - 1
    received, kept = [], []
    tail = (QUARTER, SUB, 4 * SUB)
    for order in stage_shapes(workers):
        for step in range(bits):
            count = workers >> step
            low = 1 << order[step]
            received.append(pltpu.VMEM((CH, count // (2 * low), low) + tail, jnp.float32))
            if step < bits - 1:
                low = 1 << order[step + 1]
                kept.append(pltpu.VMEM((CH, count // 2 // (2 * low), 2, low) + tail, jnp.float32))
            else:
                kept.append(pltpu.VMEM((CH,) + tail, jnp.float32))
    columns, rows = transform_matrices()
    vmem = pl.BlockSpec(memory_space=pltpu.VMEM)
    return pl.pallas_call(
        functools.partial(combine_kernel, workers, tiles),
        out_shape=jax.ShapeDtypeStruct((2 * CH, height, GCW), jnp.float32),
        in_specs=[pl.BlockSpec(memory_space=pltpu.SMEM), vmem, vmem, vmem],
        out_specs=vmem,
        scratch_shapes=received + kept + [
            pltpu.VMEM((2 * CH, SUBW * SUB, 2 * GCW), jnp.bfloat16),
            pltpu.VMEM((CH, tiles - 1, 2, height, GCW), jnp.float32),
            pltpu.VMEM((CH, tiles - 1, 2, height, GCW), jnp.float32),
            pltpu.SemaphoreType.DMA((CH, 2, bits)),
            pltpu.SemaphoreType.DMA((CH, 2, bits)),
            pltpu.SemaphoreType.DMA((CH, tiles - 1)),
            pltpu.SemaphoreType.DMA((CH, tiles - 1)),
        ],
        compiler_params=pltpu.CompilerParams(
            collective_id=0, has_side_effects=True, vmem_limit_bytes=48 * 1024 * 1024
        ),
        name="reduce_and_place",
    )(
        jnp.transpose(corners),
        pictures.reshape(CH, workers // 2, 2, 1, 2 * QUARTER, SUB, 4 * SUB),
        jnp.asarray(columns),
        jnp.asarray(rows),
    )


def local(height, block_coords, block_visibilities, subgrid_of_block, live_blocks, corners, channel_scale):
    workers = lax.axis_size("work")
    tiles = lax.axis_size("tile")
    pictures = partial_pictures(
        jnp.transpose(block_coords, (1, 0, 2)), block_visibilities, subgrid_of_block, live_blocks, channel_scale, corners.shape[0]
    )
    return combine(pictures, corners, workers, tiles, height)


def solution(mesh):
    height = 64
    return jax.shard_map(
        functools.partial(local, height),
        mesh=mesh,
        in_specs=(
            P(("work", "tile"), None, None),
            P(("work", "tile"), None, None),
            P(("work", "tile")),
            P(("work", "tile")),
            P(),
            P(),
        ),
        out_specs=P(None, "tile", "work"),
        check_vma=False,
    )
```

```python
import functools
import math

import jax
import jax.numpy as jnp
import numpy as np
from jax import lax
from jax.experimental import pallas as pl
from jax.experimental.pallas import tpu as pltpu
from jax.sharding import PartitionSpec as P

CH = 2
SUB = 32
ROWS = 128
GCW = 128
SUBW = 16
FOLD = SUB // 2
HALF = FOLD // 2
UNROLL = 4
MESH = pl.DeviceIdType.MESH
highest = lax.Precision.HIGHEST

NEAREST = 12582912.0
SIN = (6.283184916495431, -41.34158923268848, 81.59994332978006, -76.61447253122435, 41.34288235446963, -12.471243534886277)
COS = (0.9999992107823215, -19.73898035576396, 64.92865742103214, -85.2716215342875, 58.7904921200778, -21.07110562755528)


def horner(coefficients, z):
    total = jnp.full_like(z, coefficients[-1])
    for value in coefficients[-2::-1]:
        total = total * z + value
    return total


def sincos_turns(turns):
    rest = turns - ((turns + NEAREST) - NEAREST)
    z = rest * rest
    return rest * horner(SIN, z), horner(COS, z)


def split(value):
    high = value.astype(jnp.bfloat16)
    return high, (value - high.astype(jnp.float32)).astype(jnp.bfloat16)


def dot_nt(left, right):
    return lax.dot_general(left, right, (((1,), (1,)), ((), ())), preferred_element_type=jnp.float32)


def transform_matrices():
    at = np.arange(SUB)
    taper = np.sin(np.pi * (at + 0.5) / SUB) ** 2
    angles = 2.0 * math.pi * (at[:, None] * at[None, :] % SUB) / SUB
    real, imag = taper[:, None] * np.cos(angles), -taper[:, None] * np.sin(angles)
    plain = np.block([[real, imag], [-imag, real]])
    turned = np.block([[-imag, real], [-real, -imag]])
    columns = np.kron(np.eye(2), np.concatenate([plain, turned], axis=1))
    rows = np.concatenate([real.T, imag.T], axis=1) / (ROWS * SUB)
    return columns.astype(np.float32), rows.astype(np.float32)


def stage_shapes(workers):
    bits = workers.bit_length() - 1
    return [[0] * bits, [0] + [bits - 1 - step for step in range(1, bits)]]


def grid_kernel(workers, tiles, *refs):
    live_ref, scale_ref, corners_ref, labels_ref, coords_ref, waves_ref, columns_ref, rows_ref, out_ref = refs[:9]
    bits = workers.bit_length() - 1
    orders = stage_shapes(workers)
    scratch = list(refs[9:])
    received = [[scratch.pop(0) for _ in range(bits)] for _ in range(2)]
    kept = [[scratch.pop(0) for _ in range(bits)] for _ in range(2)]
    pictures_ref, data_ref, first_ref, placed, outgoing, incoming, send_sem, recv_sem, tile_send, tile_recv = scratch
    worker, tile = lax.axis_index("work"), lax.axis_index("tile")
    height = out_ref.shape[1]

    def partner(bit):
        return worker + (1 << bit) * (1 - 2 * ((worker >> bit) & 1))

    barrier = pltpu.get_barrier_semaphore()
    for bit in range(bits):
        pl.semaphore_signal(barrier, inc=1, device_id=(partner(bit), tile), device_id_type=MESH)
    for far in range(1, tiles):
        pl.semaphore_signal(barrier, inc=1, device_id=(worker, lax.rem(tile + far, tiles)), device_id_type=MESH)

    def own_part(channel, half, step):
        if step == 0:
            return data_ref.at[channel], pl.ds(half * HALF, HALF)
        return kept[half][step - 1].at[channel], slice(None)

    def halved_bit(half, step):
        return 0 if step == 0 else (step if half == 0 else bits - step)

    def step_copy(channel, half, step):
        bit = halved_bit(half, step)
        source, pairs = own_part(channel, half, step)
        return pltpu.make_async_remote_copy(
            src_ref=source.at[:, 1 - ((worker >> bit) & 1), :, pairs],
            dst_ref=received[half][step].at[channel],
            send_sem=send_sem.at[channel, half, step],
            recv_sem=recv_sem.at[channel, half, step],
            device_id=(partner(bit), tile),
            device_id_type=MESH,
        )

    def step_sum(channel, half, step):
        mine = (worker >> halved_bit(half, step)) & 1
        source, pairs = own_part(channel, half, step)
        arrived = received[half][step].at[channel]
        target = kept[half][step].at[channel]
        if step == bits - 1:
            target[...] = source[0, mine, 0, pairs] + arrived[0, 0]
            return
        low, low_next = arrived.shape[1], target.shape[2]
        for a in range(arrived.shape[0]):
            for b in range(low):
                at = a * low + b
                target[at // (2 * low_next), at // low_next % 2, at % low_next] = source[a, mine, b, pairs] + arrived[a, b]

    copies = {}

    def advance(channel, step):
        for half in range(2):
            copies[channel, half].wait()
            step_sum(channel, half, step)
            if step < bits - 1:
                copies[channel, half] = step_copy(channel, half, step + 1)
                copies[channel, half].start()

    width = 4 * SUB
    columns, rows = columns_ref[...], rows_ref[...]
    lane = lax.broadcasted_iota(jnp.int32, (1, SUBW * SUB), 1)
    row_at = lane % SUB
    for s in range(SUBW):
        row_at = row_at + jnp.where(lane // SUB == s, corners_ref[0, worker * SUBW + s], 0)
    stripe = lax.broadcasted_iota(jnp.int32, (width, GCW), 0)
    across = lax.broadcasted_iota(jnp.int32, (width, GCW), 1) - stripe % SUB
    group = lax.broadcasted_iota(jnp.int32, (width, width), 0) // SUB
    same = group == lax.broadcasted_iota(jnp.int32, (width, width), 1) // SUB

    low_lanes = lax.broadcasted_iota(jnp.int32, (SUB, width), 1) < 2 * SUB

    def transform(channel):
        pictures = jnp.concatenate(
            [kept[half][bits - 1][channel].reshape(HALF * SUBW, width) for half in range(2)], axis=0
        )
        first = jnp.dot(pictures, columns, precision=highest, preferred_element_type=jnp.float32)
        first_ref[0] = first[:, :width]
        first_ref[1] = first[:, width:]
        plain, turned = [], []
        for j in range(SUBW // 2):
            even, odd = [
                jnp.concatenate(
                    [first_ref[side, pl.ds(2 * j + s, FOLD, stride=SUBW), :] for side in range(2)], axis=0
                )
                for s in range(2)
            ]
            plain.append(jnp.where(low_lanes, even, pltpu.roll(odd, 2 * SUB, 1)))
            turned.append(jnp.where(low_lanes, pltpu.roll(even, 2 * SUB, 1), odd))
        stacked = jnp.concatenate([jnp.concatenate(plain, axis=1), jnp.concatenate(turned, axis=1)], axis=0)
        spectra = jnp.dot(rows, stacked, precision=highest, preferred_element_type=jnp.float32)
        for j in range(SUBW // 2):
            spectrum = spectra[:, j * width:(j + 1) * width]
            spread = jnp.where(same, jnp.concatenate([spectrum] * 4, axis=0), 0.0)
            high, low = split(spread)
            column = [corners_ref[1, worker * SUBW + 2 * j + side] - worker * GCW for side in range(2)]
            target = across == jnp.where(stripe < 2 * SUB, column[0], column[1])
            target = jnp.where(target, 1.0, 0.0).astype(jnp.bfloat16)
            wide = jnp.dot(jnp.concatenate([high, low], axis=0), target, preferred_element_type=jnp.float32)
            high, low = split(wide[:width] + wide[width:])
            for side in range(2):
                for part in range(2):
                    here = slice((2 * side + part) * SUB, (2 * side + part + 1) * SUB)
                    there = slice((2 * j + side) * SUB, (2 * j + side + 1) * SUB)
                    placed[2 * channel + part, there, :GCW] = high[here]
                    placed[2 * channel + part, there, GCW:] = low[here]

    def tile_rows(channel, which, store):
        line = lax.broadcasted_iota(jnp.int32, (height, SUBW * SUB), 0) + which * height
        select = jnp.where(line == row_at, 1.0, 0.0).astype(jnp.bfloat16)
        for part in range(2):
            both = jnp.dot(select, placed[2 * channel + part], preferred_element_type=jnp.float32)
            store[part] = both[:, :GCW] + both[:, GCW:]

    blocks = waves_ref.shape[0]
    steps = blocks // UNROLL
    offset = (lax.broadcasted_iota(jnp.int32, (SUB, ROWS), 0) - SUB // 2).astype(jnp.float32) * (1.0 / SUB)
    square = offset * offset
    low_half = lax.broadcasted_iota(jnp.int32, (FOLD, width), 1) < 2 * SUB

    def picture(channel, block):
        first, second, third = [coords_ref[axis, pl.ds(block, 1), :] for axis in range(3)]
        waves = waves_ref[block]
        factor = scale_ref[channel]
        depth = third * square
        sine, cosine = sincos_turns((first * offset + depth) * factor)
        real, imag = waves[2 * channel:2 * channel + 1, :], waves[2 * channel + 1:2 * channel + 2, :]
        left_high, left_low = split(
            jnp.concatenate([real * cosine - imag * sine, real * sine + imag * cosine], axis=1)
        )
        sine, cosine = sincos_turns((second * offset + depth) * factor)
        sine_high, sine_low = split(sine)
        cosine_high, cosine_low = split(cosine)
        right = jnp.concatenate(
            [
                jnp.concatenate([cosine_high, -sine_high], axis=1),
                jnp.concatenate([sine_high, cosine_high], axis=1),
                jnp.concatenate([cosine_low, -sine_low], axis=1),
                jnp.concatenate([sine_low, cosine_low], axis=1),
            ],
            axis=0,
        )
        product = dot_nt(jnp.concatenate([left_high, left_low], axis=0), right)
        product = product[:SUB] + product[SUB:]
        product = product + pltpu.roll(product, 2 * SUB, 1)
        return jnp.where(low_half, product[:FOLD], product[FOLD:])

    def fill(channel, begin, end):
        def body(step, carry):
            base = step * UNROLL
            group = [picture(channel, base + k) for k in range(UNROLL)]
            for k in range(UNROLL):
                pictures_ref[pl.ds(base + k, FOLD, stride=blocks), :] = group[k]
            return carry

        lax.fori_loop(begin, end, body, 0)

    def merge(channel):
        subgrids = SUBW * workers
        named = lax.broadcasted_iota(jnp.int32, (subgrids, blocks), 0) == labels_ref[...]
        alive = lax.broadcasted_iota(jnp.int32, (subgrids, blocks), 1) < live_ref[0]
        choose = jnp.where(named & alive, 1.0, 0.0).astype(jnp.bfloat16)
        for x in range(FOLD):
            high, low = split(pictures_ref[x * blocks:(x + 1) * blocks])
            both = jnp.dot(choose, jnp.concatenate([high, low], axis=1), preferred_element_type=jnp.float32)
            both = both[:, :width] + both[:, width:]
            for w in range(workers):
                data_ref[channel, w // 2, w % 2, 0, x] = both[w * SUBW:(w + 1) * SUBW]

    def begin(channel):
        for half in range(2):
            copies[channel, half] = step_copy(channel, half, 0)
            copies[channel, half].start()

    sent = []

    def spread_tiles(channel):
        for far in range(tiles - 1, 0, -1):
            which = lax.rem(tile + far, tiles)
            tile_rows(channel, which, outgoing.at[channel, far - 1])
            copy = pltpu.make_async_remote_copy(
                src_ref=outgoing.at[channel, far - 1],
                dst_ref=incoming.at[channel, far - 1],
                send_sem=tile_send.at[channel, far - 1],
                recv_sem=tile_recv.at[channel, far - 1],
                device_id=(worker, which),
                device_id_type=MESH,
            )
            copy.start()
            sent.append(copy)
        tile_rows(channel, tile, out_ref.at[pl.ds(2 * channel, 2)])

    fill(0, 0, steps)
    merge(0)
    pl.semaphore_wait(barrier, bits + tiles - 1)
    begin(0)
    done = 0
    for step in range(bits):
        until = steps * (2 * step + 1) // (2 * bits + 1)
        fill(1, done, until)
        done = until
        advance(0, step)
    transform(0)
    spread_tiles(0)
    fill(1, done, steps)
    merge(1)
    begin(1)
    for step in range(bits):
        advance(1, step)
    transform(1)
    spread_tiles(1)
    for copy in sent:
        copy.wait()
    for channel in range(CH):
        total = out_ref[2 * channel:2 * channel + 2]
        for far in range(tiles - 1):
            total = total + incoming[channel, far]
        out_ref[2 * channel:2 * channel + 2] = total


def gridded(coords, waves, labels, live, corners, scale, workers, tiles, height):
    bits = workers.bit_length() - 1
    blocks = waves.shape[0]
    width = 4 * SUB
    received, kept = [], []
    tail = (HALF, SUBW, width)
    for order in stage_shapes(workers):
        for step in range(bits):
            count = workers >> step
            low = 1 << order[step]
            received.append(pltpu.VMEM((CH, count // (2 * low), low) + tail, jnp.float32))
            if step < bits - 1:
                low = 1 << order[step + 1]
                kept.append(pltpu.VMEM((CH, count // 2 // (2 * low), 2, low) + tail, jnp.float32))
            else:
                kept.append(pltpu.VMEM((CH,) + tail, jnp.float32))
    columns, rows = transform_matrices()
    vmem = pl.BlockSpec(memory_space=pltpu.VMEM)
    smem = pl.BlockSpec(memory_space=pltpu.SMEM)
    return pl.pallas_call(
        functools.partial(grid_kernel, workers, tiles),
        out_shape=jax.ShapeDtypeStruct((2 * CH, height, GCW), jnp.float32),
        in_specs=[smem, smem, smem, vmem, vmem, vmem, vmem, vmem],
        out_specs=vmem,
        scratch_shapes=received + kept + [
            pltpu.VMEM((FOLD * blocks, width), jnp.float32),
            pltpu.VMEM((CH, workers // 2, 2, 1, FOLD, SUBW, width), jnp.float32),
            pltpu.VMEM((2, FOLD * SUBW, width), jnp.float32),
            pltpu.VMEM((2 * CH, SUBW * SUB, 2 * GCW), jnp.bfloat16),
            pltpu.VMEM((CH, tiles - 1, 2, height, GCW), jnp.float32),
            pltpu.VMEM((CH, tiles - 1, 2, height, GCW), jnp.float32),
            pltpu.SemaphoreType.DMA((CH, 2, bits)),
            pltpu.SemaphoreType.DMA((CH, 2, bits)),
            pltpu.SemaphoreType.DMA((CH, tiles - 1)),
            pltpu.SemaphoreType.DMA((CH, tiles - 1)),
        ],
        compiler_params=pltpu.CompilerParams(
            collective_id=0, has_side_effects=True, vmem_limit_bytes=56 * 1024 * 1024
        ),
        name="grid_blocks",
    )(live, scale, jnp.transpose(corners), labels.reshape(1, blocks), coords, waves, jnp.asarray(columns), jnp.asarray(rows))


def local(height, block_coords, block_visibilities, subgrid_of_block, live_blocks, corners, channel_scale):
    workers = lax.axis_size("work")
    tiles = lax.axis_size("tile")
    return gridded(
        jnp.transpose(block_coords, (1, 0, 2)), block_visibilities, subgrid_of_block, live_blocks, corners,
        channel_scale, workers, tiles, height,
    )


def solution(mesh):
    height = 64
    return jax.shard_map(
        functools.partial(local, height),
        mesh=mesh,
        in_specs=(
            P(("work", "tile"), None, None),
            P(("work", "tile"), None, None),
            P(("work", "tile")),
            P(("work", "tile")),
            P(),
            P(),
        ),
        out_specs=P(None, "tile", "work"),
        check_vma=False,
    )
```

```python
import functools
import math

import jax
import jax.numpy as jnp
import numpy as np
from jax import lax
from jax.experimental import pallas as pl
from jax.experimental.pallas import tpu as pltpu
from jax.sharding import PartitionSpec as P

CH = 2
SUB = 32
ROWS = 128
GCW = 128
SUBW = 16
FOLD = SUB // 2
HALF = FOLD // 2
UNROLL = 16
MESH = pl.DeviceIdType.MESH
highest = lax.Precision.HIGHEST

NEAREST = 12582912.0
SIN = (6.283184916495431, -41.34158923268848, 81.59994332978006, -76.61447253122435, 41.34288235446963, -12.471243534886277)
COS = (0.9999992107823215, -19.73898035576396, 64.92865742103214, -85.2716215342875, 58.7904921200778, -21.07110562755528)


def horner(coefficients, z):
    total = jnp.full_like(z, coefficients[-1])
    for value in coefficients[-2::-1]:
        total = total * z + value
    return total


def sincos_turns(turns):
    rest = turns - ((turns + NEAREST) - NEAREST)
    z = rest * rest
    return rest * horner(SIN, z), horner(COS, z)


def split(value):
    high = value.astype(jnp.bfloat16)
    return high, (value - high.astype(jnp.float32)).astype(jnp.bfloat16)


def dot_nt(left, right):
    return lax.dot_general(left, right, (((1,), (1,)), ((), ())), preferred_element_type=jnp.float32)


def transform_matrices():
    at = np.arange(SUB)
    taper = np.sin(np.pi * (at + 0.5) / SUB) ** 2
    angles = 2.0 * math.pi * (at[:, None] * at[None, :] % SUB) / SUB
    real, imag = taper[:, None] * np.cos(angles), -taper[:, None] * np.sin(angles)
    plain = np.block([[real, imag], [-imag, real]])
    turned = np.block([[-imag, real], [-real, -imag]])
    columns = np.kron(np.eye(2), np.concatenate([plain, turned], axis=1))
    rows = np.concatenate([real.T, imag.T], axis=1) / (ROWS * SUB)
    return columns.astype(np.float32), rows.astype(np.float32)


def stage_shapes(workers):
    bits = workers.bit_length() - 1
    return [[0] * bits, [0] + [bits - 1 - step for step in range(1, bits)]]


def grid_kernel(workers, tiles, *refs):
    live_ref, scale_ref, corners_ref, labels_ref, coords_ref, waves_ref, columns_ref, rows_ref, out_ref = refs[:9]
    bits = workers.bit_length() - 1
    orders = stage_shapes(workers)
    scratch = list(refs[9:])
    received = [[scratch.pop(0) for _ in range(bits)] for _ in range(2)]
    kept = [[scratch.pop(0) for _ in range(bits)] for _ in range(2)]
    pictures_ref, data_ref, first_ref, placed, outgoing, incoming, send_sem, recv_sem, tile_send, tile_recv = scratch
    worker, tile = lax.axis_index("work"), lax.axis_index("tile")
    height = out_ref.shape[1]

    def partner(bit):
        return worker + (1 << bit) * (1 - 2 * ((worker >> bit) & 1))

    barrier = pltpu.get_barrier_semaphore()
    for bit in range(bits):
        pl.semaphore_signal(barrier, inc=1, device_id=(partner(bit), tile), device_id_type=MESH)
    for far in range(1, tiles):
        pl.semaphore_signal(barrier, inc=1, device_id=(worker, lax.rem(tile + far, tiles)), device_id_type=MESH)

    def own_part(channel, half, step):
        if step == 0:
            return data_ref.at[channel], pl.ds(half * HALF, HALF)
        return kept[half][step - 1].at[channel], slice(None)

    def halved_bit(half, step):
        return 0 if step == 0 else (step if half == 0 else bits - step)

    def step_copy(channel, half, step):
        bit = halved_bit(half, step)
        source, pairs = own_part(channel, half, step)
        return pltpu.make_async_remote_copy(
            src_ref=source.at[:, 1 - ((worker >> bit) & 1), :, pairs],
            dst_ref=received[half][step].at[channel],
            send_sem=send_sem.at[channel, half, step],
            recv_sem=recv_sem.at[channel, half, step],
            device_id=(partner(bit), tile),
            device_id_type=MESH,
        )

    def step_sum(channel, half, step):
        mine = (worker >> halved_bit(half, step)) & 1
        source, pairs = own_part(channel, half, step)
        arrived = received[half][step].at[channel]
        target = kept[half][step].at[channel]
        if step == bits - 1:
            target[...] = source[0, mine, 0, pairs] + arrived[0, 0]
            return
        low, low_next = arrived.shape[1], target.shape[2]
        for a in range(arrived.shape[0]):
            for b in range(low):
                at = a * low + b
                target[at // (2 * low_next), at // low_next % 2, at % low_next] = source[a, mine, b, pairs] + arrived[a, b]

    copies = {}

    def advance(channel, step):
        for half in range(2):
            copies[channel, half].wait()
            step_sum(channel, half, step)
            if step < bits - 1:
                copies[channel, half] = step_copy(channel, half, step + 1)
                copies[channel, half].start()

    width = 4 * SUB
    columns, rows = columns_ref[...], rows_ref[...]
    lane = lax.broadcasted_iota(jnp.int32, (1, SUBW * SUB), 1)
    row_at = lane % SUB
    for s in range(SUBW):
        row_at = row_at + jnp.where(lane // SUB == s, corners_ref[0, worker * SUBW + s], 0)
    stripe = lax.broadcasted_iota(jnp.int32, (width, GCW), 0)
    across = lax.broadcasted_iota(jnp.int32, (width, GCW), 1) - stripe % SUB
    group = lax.broadcasted_iota(jnp.int32, (width, width), 0) // SUB
    same = group == lax.broadcasted_iota(jnp.int32, (width, width), 1) // SUB

    low_lanes = lax.broadcasted_iota(jnp.int32, (SUB, width), 1) < 2 * SUB

    def transform(channel):
        pictures = jnp.concatenate(
            [kept[half][bits - 1][channel].reshape(HALF * SUBW, width) for half in range(2)], axis=0
        )
        first = jnp.dot(pictures, columns, precision=highest, preferred_element_type=jnp.float32)
        first_ref[0] = first[:, :width]
        first_ref[1] = first[:, width:]
        plain, turned = [], []
        for j in range(SUBW // 2):
            even, odd = [
                jnp.concatenate(
                    [first_ref[side, pl.ds(2 * j + s, FOLD, stride=SUBW), :] for side in range(2)], axis=0
                )
                for s in range(2)
            ]
            plain.append(jnp.where(low_lanes, even, pltpu.roll(odd, 2 * SUB, 1)))
            turned.append(jnp.where(low_lanes, pltpu.roll(even, 2 * SUB, 1), odd))
        stacked = jnp.concatenate([jnp.concatenate(plain, axis=1), jnp.concatenate(turned, axis=1)], axis=0)
        spectra = jnp.dot(rows, stacked, precision=highest, preferred_element_type=jnp.float32)
        for j in range(SUBW // 2):
            spectrum = spectra[:, j * width:(j + 1) * width]
            spread = jnp.where(same, jnp.concatenate([spectrum] * 4, axis=0), 0.0)
            high, low = split(spread)
            column = [corners_ref[1, worker * SUBW + 2 * j + side] - worker * GCW for side in range(2)]
            target = across == jnp.where(stripe < 2 * SUB, column[0], column[1])
            target = jnp.where(target, 1.0, 0.0).astype(jnp.bfloat16)
            wide = jnp.dot(jnp.concatenate([high, low], axis=0), target, preferred_element_type=jnp.float32)
            high, low = split(wide[:width] + wide[width:])
            for side in range(2):
                for part in range(2):
                    here = slice((2 * side + part) * SUB, (2 * side + part + 1) * SUB)
                    there = slice((2 * j + side) * SUB, (2 * j + side + 1) * SUB)
                    placed[2 * channel + part, there, :GCW] = high[here]
                    placed[2 * channel + part, there, GCW:] = low[here]

    def tile_rows(channel, which, store):
        line = lax.broadcasted_iota(jnp.int32, (height, SUBW * SUB), 0) + which * height
        select = jnp.where(line == row_at, 1.0, 0.0).astype(jnp.bfloat16)
        for part in range(2):
            both = jnp.dot(select, placed[2 * channel + part], preferred_element_type=jnp.float32)
            store[part] = both[:, :GCW] + both[:, GCW:]

    blocks = waves_ref.shape[0]
    steps = blocks // UNROLL
    offset = (lax.broadcasted_iota(jnp.int32, (SUB, ROWS), 0) - SUB // 2).astype(jnp.float32) * (1.0 / SUB)
    square = offset * offset
    low_half = lax.broadcasted_iota(jnp.int32, (FOLD, width), 1) < 2 * SUB

    def picture(channel, block):
        first, second, third = [coords_ref[axis, pl.ds(block, 1), :] for axis in range(3)]
        waves = waves_ref[block]
        factor = scale_ref[channel]
        depth = third * square
        sine, cosine = sincos_turns((first * offset + depth) * factor)
        real, imag = waves[2 * channel:2 * channel + 1, :], waves[2 * channel + 1:2 * channel + 2, :]
        left_high, left_low = split(
            jnp.concatenate([real * cosine - imag * sine, real * sine + imag * cosine], axis=1)
        )
        sine, cosine = sincos_turns((second * offset + depth) * factor)
        sine_high, sine_low = split(sine)
        cosine_high, cosine_low = split(cosine)
        right = jnp.concatenate(
            [
                jnp.concatenate([cosine_high, -sine_high], axis=1),
                jnp.concatenate([sine_high, cosine_high], axis=1),
                jnp.concatenate([cosine_low, -sine_low], axis=1),
                jnp.concatenate([sine_low, cosine_low], axis=1),
            ],
            axis=0,
        )
        product = dot_nt(jnp.concatenate([left_high, left_low], axis=0), right)
        product = product[:SUB] + product[SUB:]
        product = product + pltpu.roll(product, 2 * SUB, 1)
        return jnp.where(low_half, product[:FOLD], product[FOLD:])

    def fill(channel, begin, end):
        def body(step, carry):
            base = step * UNROLL
            group = [picture(channel, base + k) for k in range(UNROLL)]
            for k in range(UNROLL):
                pictures_ref[pl.ds(base + k, FOLD, stride=blocks), :] = group[k]
            return carry

        lax.fori_loop(begin, end, body, 0)

    def merge(channel):
        subgrids = SUBW * workers
        named = lax.broadcasted_iota(jnp.int32, (subgrids, blocks), 0) == labels_ref[...]
        alive = lax.broadcasted_iota(jnp.int32, (subgrids, blocks), 1) < live_ref[0]
        choose = jnp.where(named & alive, 1.0, 0.0).astype(jnp.bfloat16)
        for x in range(FOLD):
            high, low = split(pictures_ref[x * blocks:(x + 1) * blocks])
            both = jnp.dot(choose, jnp.concatenate([high, low], axis=1), preferred_element_type=jnp.float32)
            both = both[:, :width] + both[:, width:]
            for w in range(workers):
                data_ref[channel, w // 2, w % 2, 0, x] = both[w * SUBW:(w + 1) * SUBW]

    def begin(channel):
        for half in range(2):
            copies[channel, half] = step_copy(channel, half, 0)
            copies[channel, half].start()

    sent = []

    def spread_tiles(channel):
        for far in range(tiles - 1, 0, -1):
            which = lax.rem(tile + far, tiles)
            tile_rows(channel, which, outgoing.at[channel, far - 1])
            copy = pltpu.make_async_remote_copy(
                src_ref=outgoing.at[channel, far - 1],
                dst_ref=incoming.at[channel, far - 1],
                send_sem=tile_send.at[channel, far - 1],
                recv_sem=tile_recv.at[channel, far - 1],
                device_id=(worker, which),
                device_id_type=MESH,
            )
            copy.start()
            sent.append(copy)
        tile_rows(channel, tile, out_ref.at[pl.ds(2 * channel, 2)])

    fill(0, 0, steps)
    merge(0)
    pl.semaphore_wait(barrier, bits + tiles - 1)
    begin(0)
    done = 0
    for step in range(bits):
        until = steps - (4 * steps // 5 >> step)
        fill(1, done, until)
        done = until
        advance(0, step)
    transform(0)
    spread_tiles(0)
    fill(1, done, steps)
    merge(1)
    begin(1)
    for step in range(bits):
        advance(1, step)
    transform(1)
    spread_tiles(1)
    for copy in sent:
        copy.wait()
    for channel in range(CH):
        total = out_ref[2 * channel:2 * channel + 2]
        for far in range(tiles - 1):
            total = total + incoming[channel, far]
        out_ref[2 * channel:2 * channel + 2] = total


def gridded(coords, waves, labels, live, corners, scale, workers, tiles, height):
    bits = workers.bit_length() - 1
    blocks = waves.shape[0]
    width = 4 * SUB
    received, kept = [], []
    tail = (HALF, SUBW, width)
    for order in stage_shapes(workers):
        for step in range(bits):
            count = workers >> step
            low = 1 << order[step]
            received.append(pltpu.VMEM((CH, count // (2 * low), low) + tail, jnp.float32))
            if step < bits - 1:
                low = 1 << order[step + 1]
                kept.append(pltpu.VMEM((CH, count // 2 // (2 * low), 2, low) + tail, jnp.float32))
            else:
                kept.append(pltpu.VMEM((CH,) + tail, jnp.float32))
    columns, rows = transform_matrices()
    vmem = pl.BlockSpec(memory_space=pltpu.VMEM)
    smem = pl.BlockSpec(memory_space=pltpu.SMEM)
    return pl.pallas_call(
        functools.partial(grid_kernel, workers, tiles),
        out_shape=jax.ShapeDtypeStruct((2 * CH, height, GCW), jnp.float32),
        in_specs=[smem, smem, smem, vmem, vmem, vmem, vmem, vmem],
        out_specs=vmem,
        scratch_shapes=received + kept + [
            pltpu.VMEM((FOLD * blocks, width), jnp.float32),
            pltpu.VMEM((CH, workers // 2, 2, 1, FOLD, SUBW, width), jnp.float32),
            pltpu.VMEM((2, FOLD * SUBW, width), jnp.float32),
            pltpu.VMEM((2 * CH, SUBW * SUB, 2 * GCW), jnp.bfloat16),
            pltpu.VMEM((CH, tiles - 1, 2, height, GCW), jnp.float32),
            pltpu.VMEM((CH, tiles - 1, 2, height, GCW), jnp.float32),
            pltpu.SemaphoreType.DMA((CH, 2, bits)),
            pltpu.SemaphoreType.DMA((CH, 2, bits)),
            pltpu.SemaphoreType.DMA((CH, tiles - 1)),
            pltpu.SemaphoreType.DMA((CH, tiles - 1)),
        ],
        compiler_params=pltpu.CompilerParams(
            collective_id=0, has_side_effects=True, vmem_limit_bytes=56 * 1024 * 1024
        ),
        name="grid_blocks",
    )(live, scale, jnp.transpose(corners), labels.reshape(1, blocks), coords, waves, jnp.asarray(columns), jnp.asarray(rows))


def local(height, block_coords, block_visibilities, subgrid_of_block, live_blocks, corners, channel_scale):
    workers = lax.axis_size("work")
    tiles = lax.axis_size("tile")
    return gridded(
        jnp.transpose(block_coords, (1, 0, 2)), block_visibilities, subgrid_of_block, live_blocks, corners,
        channel_scale, workers, tiles, height,
    )


def solution(mesh):
    height = 64
    return jax.shard_map(
        functools.partial(local, height),
        mesh=mesh,
        in_specs=(
            P(("work", "tile"), None, None),
            P(("work", "tile"), None, None),
            P(("work", "tile")),
            P(("work", "tile")),
            P(),
            P(),
        ),
        out_specs=P(None, "tile", "work"),
        check_vma=False,
    )
```

```python
import functools
import math

import jax
import jax.numpy as jnp
import numpy as np
from jax import lax
from jax.experimental import pallas as pl
from jax.experimental.pallas import tpu as pltpu
from jax.sharding import PartitionSpec as P

CH = 2
SUB = 32
ROWS = 128
GCW = 128
SUBW = 16
FOLD = SUB // 2
HALF = FOLD // 2
UNROLL = 16
MESH = pl.DeviceIdType.MESH
highest = lax.Precision.HIGHEST

NEAREST = 12582912.0
SIN = (4.442882919124344, -7.308245686508998, 3.606354218431858, -0.8461116503680876, 0.10982451641509068)
COS = (1.4142134962552282, -6.978850948563766, 5.73946037690631, -1.8835579059813616, 0.31068802751622054)


def horner(coefficients, z):
    total = jnp.full_like(z, coefficients[-1])
    for value in coefficients[-2::-1]:
        total = total * z + value
    return total


def sincos_turns(turns):
    rest = turns - ((turns + NEAREST) - NEAREST)
    z = rest * rest
    half = rest * horner(SIN, z)
    return half * horner(COS, z), 1.0 - half * half


def split(value):
    high = value.astype(jnp.bfloat16)
    return high, (value - high.astype(jnp.float32)).astype(jnp.bfloat16)


def dot_nt(left, right):
    return lax.dot_general(left, right, (((1,), (1,)), ((), ())), preferred_element_type=jnp.float32)


def transform_matrices():
    at = np.arange(SUB)
    taper = np.sin(np.pi * (at + 0.5) / SUB) ** 2
    angles = 2.0 * math.pi * (at[:, None] * at[None, :] % SUB) / SUB
    real, imag = taper[:, None] * np.cos(angles), -taper[:, None] * np.sin(angles)
    plain = np.block([[real, imag], [-imag, real]])
    turned = np.block([[-imag, real], [-real, -imag]])
    columns = np.kron(np.eye(2), np.concatenate([plain, turned], axis=1))
    rows = np.concatenate([real.T, imag.T], axis=1) / (ROWS * SUB)
    return columns.astype(np.float32), rows.astype(np.float32)


def stage_shapes(workers):
    bits = workers.bit_length() - 1
    return [[0] * bits, [0] + [bits - 1 - step for step in range(1, bits)]]


def grid_kernel(workers, tiles, *refs):
    live_ref, scale_ref, corners_ref, labels_ref, coords_ref, waves_ref, columns_ref, rows_ref, out_ref = refs[:9]
    bits = workers.bit_length() - 1
    orders = stage_shapes(workers)
    scratch = list(refs[9:])
    received = [[scratch.pop(0) for _ in range(bits)] for _ in range(2)]
    kept = [[scratch.pop(0) for _ in range(bits)] for _ in range(2)]
    pictures_ref, data_ref, first_ref, placed, outgoing, incoming, send_sem, recv_sem, tile_send, tile_recv = scratch
    worker, tile = lax.axis_index("work"), lax.axis_index("tile")
    height = out_ref.shape[1]

    def partner(bit):
        return worker + (1 << bit) * (1 - 2 * ((worker >> bit) & 1))

    barrier = pltpu.get_barrier_semaphore()
    for bit in range(bits):
        pl.semaphore_signal(barrier, inc=1, device_id=(partner(bit), tile), device_id_type=MESH)
    for far in range(1, tiles):
        pl.semaphore_signal(barrier, inc=1, device_id=(worker, lax.rem(tile + far, tiles)), device_id_type=MESH)

    def own_part(channel, half, step):
        if step == 0:
            return data_ref.at[channel], pl.ds(half * HALF, HALF)
        return kept[half][step - 1].at[channel], slice(None)

    def halved_bit(half, step):
        return 0 if step == 0 else (step if half == 0 else bits - step)

    def step_copy(channel, half, step):
        bit = halved_bit(half, step)
        source, pairs = own_part(channel, half, step)
        return pltpu.make_async_remote_copy(
            src_ref=source.at[:, 1 - ((worker >> bit) & 1), :, pairs],
            dst_ref=received[half][step].at[channel],
            send_sem=send_sem.at[channel, half, step],
            recv_sem=recv_sem.at[channel, half, step],
            device_id=(partner(bit), tile),
            device_id_type=MESH,
        )

    def step_sum(channel, half, step):
        mine = (worker >> halved_bit(half, step)) & 1
        source, pairs = own_part(channel, half, step)
        arrived = received[half][step].at[channel]
        target = kept[half][step].at[channel]
        if step == bits - 1:
            target[...] = source[0, mine, 0, pairs] + arrived[0, 0]
            return
        low, low_next = arrived.shape[1], target.shape[2]
        for a in range(arrived.shape[0]):
            for b in range(low):
                at = a * low + b
                target[at // (2 * low_next), at // low_next % 2, at % low_next] = source[a, mine, b, pairs] + arrived[a, b]

    copies = {}

    def advance(channel, step):
        for half in range(2):
            copies[channel, half].wait()
            step_sum(channel, half, step)
            if step < bits - 1:
                copies[channel, half] = step_copy(channel, half, step + 1)
                copies[channel, half].start()

    width = 4 * SUB
    columns, rows = columns_ref[...], rows_ref[...]
    lane = lax.broadcasted_iota(jnp.int32, (1, SUBW * SUB), 1)
    row_at = lane % SUB
    for s in range(SUBW):
        row_at = row_at + jnp.where(lane // SUB == s, corners_ref[0, worker * SUBW + s], 0)
    stripe = lax.broadcasted_iota(jnp.int32, (width, GCW), 0)
    across = lax.broadcasted_iota(jnp.int32, (width, GCW), 1) - stripe % SUB
    group = lax.broadcasted_iota(jnp.int32, (width, width), 0) // SUB
    same = group == lax.broadcasted_iota(jnp.int32, (width, width), 1) // SUB

    low_lanes = lax.broadcasted_iota(jnp.int32, (SUB, width), 1) < 2 * SUB

    def transform(channel):
        pictures = jnp.concatenate(
            [kept[half][bits - 1][channel].reshape(HALF * SUBW, width) for half in range(2)], axis=0
        )
        first = jnp.dot(pictures, columns, precision=highest, preferred_element_type=jnp.float32)
        first_ref[0] = first[:, :width]
        first_ref[1] = first[:, width:]
        plain, turned = [], []
        for j in range(SUBW // 2):
            even, odd = [
                jnp.concatenate(
                    [first_ref[side, pl.ds(2 * j + s, FOLD, stride=SUBW), :] for side in range(2)], axis=0
                )
                for s in range(2)
            ]
            plain.append(jnp.where(low_lanes, even, pltpu.roll(odd, 2 * SUB, 1)))
            turned.append(jnp.where(low_lanes, pltpu.roll(even, 2 * SUB, 1), odd))
        stacked = jnp.concatenate([jnp.concatenate(plain, axis=1), jnp.concatenate(turned, axis=1)], axis=0)
        spectra = jnp.dot(rows, stacked, precision=highest, preferred_element_type=jnp.float32)
        for j in range(SUBW // 2):
            spectrum = spectra[:, j * width:(j + 1) * width]
            spread = jnp.where(same, jnp.concatenate([spectrum] * 4, axis=0), 0.0)
            high, low = split(spread)
            column = [corners_ref[1, worker * SUBW + 2 * j + side] - worker * GCW for side in range(2)]
            target = across == jnp.where(stripe < 2 * SUB, column[0], column[1])
            target = jnp.where(target, 1.0, 0.0).astype(jnp.bfloat16)
            wide = jnp.dot(jnp.concatenate([high, low], axis=0), target, preferred_element_type=jnp.float32)
            high, low = split(wide[:width] + wide[width:])
            for side in range(2):
                for part in range(2):
                    here = slice((2 * side + part) * SUB, (2 * side + part + 1) * SUB)
                    there = slice((2 * j + side) * SUB, (2 * j + side + 1) * SUB)
                    placed[2 * channel + part, there, :GCW] = high[here]
                    placed[2 * channel + part, there, GCW:] = low[here]

    def tile_rows(channel, which, store):
        line = lax.broadcasted_iota(jnp.int32, (height, SUBW * SUB), 0) + which * height
        select = jnp.where(line == row_at, 1.0, 0.0).astype(jnp.bfloat16)
        for part in range(2):
            both = jnp.dot(select, placed[2 * channel + part], preferred_element_type=jnp.float32)
            store[part] = both[:, :GCW] + both[:, GCW:]

    blocks = waves_ref.shape[0]
    steps = blocks // UNROLL
    offset = (lax.broadcasted_iota(jnp.int32, (SUB, ROWS), 0) - SUB // 2).astype(jnp.float32) * (1.0 / SUB)
    square = offset * offset
    low_half = lax.broadcasted_iota(jnp.int32, (FOLD, width), 1) < 2 * SUB

    def picture(channel, block):
        factor = scale_ref[channel]
        first, second, third = [coords_ref[axis, pl.ds(block, 1), :] * factor for axis in range(3)]
        waves = waves_ref[block]
        depth = third * square
        sine, cosine = sincos_turns(first * offset + depth)
        real, imag = waves[2 * channel:2 * channel + 1, :], waves[2 * channel + 1:2 * channel + 2, :]
        left_high, left_low = split(
            jnp.concatenate([real * cosine - imag * sine, real * sine + imag * cosine], axis=1)
        )
        sine, cosine = sincos_turns(second * offset + depth)
        sine_high, sine_low = split(sine)
        cosine_high, cosine_low = split(cosine)
        right = jnp.concatenate(
            [
                jnp.concatenate([cosine_high, -sine_high], axis=1),
                jnp.concatenate([sine_high, cosine_high], axis=1),
                jnp.concatenate([cosine_low, -sine_low], axis=1),
                jnp.concatenate([sine_low, cosine_low], axis=1),
            ],
            axis=0,
        )
        product = dot_nt(jnp.concatenate([left_high, left_low], axis=0), right)
        product = product[:SUB] + product[SUB:]
        upper, lower = product[:FOLD], product[FOLD:]
        return jnp.where(low_half, upper, lower) + pltpu.roll(jnp.where(low_half, lower, upper), 2 * SUB, 1)

    def fill(channel, begin, end):
        def body(step, carry):
            base = step * UNROLL
            group = [picture(channel, base + k) for k in range(UNROLL)]
            for k in range(UNROLL):
                pictures_ref[pl.ds(base + k, FOLD, stride=blocks), :] = group[k]
            return carry

        lax.fori_loop(begin, end, body, 0)

    def merge(channel):
        subgrids = SUBW * workers
        named = lax.broadcasted_iota(jnp.int32, (subgrids, blocks), 0) == labels_ref[...]
        alive = lax.broadcasted_iota(jnp.int32, (subgrids, blocks), 1) < live_ref[0]
        choose = jnp.where(named & alive, 1.0, 0.0).astype(jnp.bfloat16)
        for half in range(2):
            for x in range(half * HALF, (half + 1) * HALF):
                high, low = split(pictures_ref[x * blocks:(x + 1) * blocks])
                both = jnp.dot(choose, jnp.concatenate([high, low], axis=1), preferred_element_type=jnp.float32)
                both = both[:, :width] + both[:, width:]
                for w in range(workers):
                    data_ref[channel, w // 2, w % 2, 0, x] = both[w * SUBW:(w + 1) * SUBW]
            if channel == 0 and half == 0:
                pl.semaphore_wait(barrier, bits + tiles - 1)
            copies[channel, half] = step_copy(channel, half, 0)
            copies[channel, half].start()

    sent = []

    def spread_tiles(channel):
        for far in range(tiles - 1, 0, -1):
            which = lax.rem(tile + far, tiles)
            tile_rows(channel, which, outgoing.at[channel, far - 1])
            copy = pltpu.make_async_remote_copy(
                src_ref=outgoing.at[channel, far - 1],
                dst_ref=incoming.at[channel, far - 1],
                send_sem=tile_send.at[channel, far - 1],
                recv_sem=tile_recv.at[channel, far - 1],
                device_id=(worker, which),
                device_id_type=MESH,
            )
            copy.start()
            sent.append(copy)
        tile_rows(channel, tile, out_ref.at[pl.ds(2 * channel, 2)])

    fill(0, 0, steps)
    merge(0)
    done = 0
    for step in range(bits):
        until = steps - (4 * steps // 5 >> step)
        fill(1, done, until)
        done = until
        advance(0, step)
    transform(0)
    spread_tiles(0)
    fill(1, done, steps)
    merge(1)
    for step in range(bits):
        advance(1, step)
    transform(1)
    spread_tiles(1)
    for copy in sent:
        copy.wait()
    for channel in range(CH):
        total = out_ref[2 * channel:2 * channel + 2]
        for far in range(tiles - 1):
            total = total + incoming[channel, far]
        out_ref[2 * channel:2 * channel + 2] = total


def gridded(coords, waves, labels, live, corners, scale, workers, tiles, height):
    bits = workers.bit_length() - 1
    blocks = waves.shape[0]
    width = 4 * SUB
    received, kept = [], []
    tail = (HALF, SUBW, width)
    for order in stage_shapes(workers):
        for step in range(bits):
            count = workers >> step
            low = 1 << order[step]
            received.append(pltpu.VMEM((CH, count // (2 * low), low) + tail, jnp.float32))
            if step < bits - 1:
                low = 1 << order[step + 1]
                kept.append(pltpu.VMEM((CH, count // 2 // (2 * low), 2, low) + tail, jnp.float32))
            else:
                kept.append(pltpu.VMEM((CH,) + tail, jnp.float32))
    columns, rows = transform_matrices()
    vmem = pl.BlockSpec(memory_space=pltpu.VMEM)
    smem = pl.BlockSpec(memory_space=pltpu.SMEM)
    return pl.pallas_call(
        functools.partial(grid_kernel, workers, tiles),
        out_shape=jax.ShapeDtypeStruct((2 * CH, height, GCW), jnp.float32),
        in_specs=[smem, smem, smem, vmem, vmem, vmem, vmem, vmem],
        out_specs=vmem,
        scratch_shapes=received + kept + [
            pltpu.VMEM((FOLD * blocks, width), jnp.float32),
            pltpu.VMEM((CH, workers // 2, 2, 1, FOLD, SUBW, width), jnp.float32),
            pltpu.VMEM((2, FOLD * SUBW, width), jnp.float32),
            pltpu.VMEM((2 * CH, SUBW * SUB, 2 * GCW), jnp.bfloat16),
            pltpu.VMEM((CH, tiles - 1, 2, height, GCW), jnp.float32),
            pltpu.VMEM((CH, tiles - 1, 2, height, GCW), jnp.float32),
            pltpu.SemaphoreType.DMA((CH, 2, bits)),
            pltpu.SemaphoreType.DMA((CH, 2, bits)),
            pltpu.SemaphoreType.DMA((CH, tiles - 1)),
            pltpu.SemaphoreType.DMA((CH, tiles - 1)),
        ],
        compiler_params=pltpu.CompilerParams(
            collective_id=0, has_side_effects=True, vmem_limit_bytes=56 * 1024 * 1024
        ),
        name="grid_blocks",
    )(live, scale, jnp.transpose(corners), labels.reshape(1, blocks), coords, waves, jnp.asarray(columns), jnp.asarray(rows))


def local(height, block_coords, block_visibilities, subgrid_of_block, live_blocks, corners, channel_scale):
    workers = lax.axis_size("work")
    tiles = lax.axis_size("tile")
    return gridded(
        jnp.transpose(block_coords, (1, 0, 2)), block_visibilities, subgrid_of_block, live_blocks, corners,
        channel_scale, workers, tiles, height,
    )


def solution(mesh):
    height = 64
    return jax.shard_map(
        functools.partial(local, height),
        mesh=mesh,
        in_specs=(
            P(("work", "tile"), None, None),
            P(("work", "tile"), None, None),
            P(("work", "tile")),
            P(("work", "tile")),
            P(),
            P(),
        ),
        out_specs=P(None, "tile", "work"),
        check_vma=False,
    )
```

```python
import functools
import math

import jax
import jax.numpy as jnp
import numpy as np
from jax import lax
from jax.experimental import pallas as pl
from jax.experimental.pallas import tpu as pltpu
from jax.sharding import PartitionSpec as P

CH = 2
SUB = 32
ROWS = 128
GCW = 128
SUBW = 16
FOLD = SUB // 2
HALF = FOLD // 2
UNROLL = 32
MESH = pl.DeviceIdType.MESH
highest = lax.Precision.HIGHEST

NEAREST = 12582912.0
SIN = (4.442882919124344, -7.308245686508998, 3.606354218431858, -0.8461116503680876, 0.10982451641509068)
COS = (1.4142134962552282, -6.978850948563766, 5.73946037690631, -1.8835579059813616, 0.31068802751622054)


def horner(coefficients, z):
    total = jnp.full_like(z, coefficients[-1])
    for value in coefficients[-2::-1]:
        total = total * z + value
    return total


def sincos_turns(turns):
    rest = turns - ((turns + NEAREST) - NEAREST)
    z = rest * rest
    half = rest * horner(SIN, z)
    return half * horner(COS, z), 1.0 - half * half


def split(value):
    high = value.astype(jnp.bfloat16)
    return high, (value - high.astype(jnp.float32)).astype(jnp.bfloat16)


def dot_nt(left, right):
    return lax.dot_general(left, right, (((1,), (1,)), ((), ())), preferred_element_type=jnp.float32)


def transform_matrices():
    at = np.arange(SUB)
    taper = np.sin(np.pi * (at + 0.5) / SUB) ** 2
    angles = 2.0 * math.pi * (at[:, None] * at[None, :] % SUB) / SUB
    real, imag = taper[:, None] * np.cos(angles), -taper[:, None] * np.sin(angles)
    plain = np.block([[real, imag], [-imag, real]])
    turned = np.block([[-imag, real], [-real, -imag]])
    columns = np.kron(np.eye(2), np.concatenate([plain, turned], axis=1))
    rows = np.concatenate([real.T, imag.T], axis=1) / (ROWS * SUB)
    return columns.astype(np.float32), rows.astype(np.float32)


def stage_shapes(workers):
    bits = workers.bit_length() - 1
    return [[0] * bits, [0] + [bits - 1 - step for step in range(1, bits)]]


def grid_kernel(workers, tiles, *refs):
    live_ref, scale_ref, corners_ref, labels_ref, coords_ref, waves_ref, columns_ref, rows_ref, out_ref = refs[:9]
    bits = workers.bit_length() - 1
    orders = stage_shapes(workers)
    scratch = list(refs[9:])
    received = [[scratch.pop(0) for _ in range(bits)] for _ in range(2)]
    kept = [[scratch.pop(0) for _ in range(bits)] for _ in range(2)]
    pictures_ref, data_ref, first_ref, placed, outgoing, incoming, send_sem, recv_sem, tile_send, tile_recv = scratch
    worker, tile = lax.axis_index("work"), lax.axis_index("tile")
    height = out_ref.shape[1]

    def partner(bit):
        return worker + (1 << bit) * (1 - 2 * ((worker >> bit) & 1))

    barrier = pltpu.get_barrier_semaphore()
    for bit in range(bits):
        pl.semaphore_signal(barrier, inc=1, device_id=(partner(bit), tile), device_id_type=MESH)
    for far in range(1, tiles):
        pl.semaphore_signal(barrier, inc=1, device_id=(worker, lax.rem(tile + far, tiles)), device_id_type=MESH)

    def own_part(channel, half, step):
        if step == 0:
            return data_ref.at[channel], pl.ds(half * HALF, HALF)
        return kept[half][step - 1].at[channel], slice(None)

    def halved_bit(half, step):
        return 0 if step == 0 else (step if half == 0 else bits - step)

    def step_copy(channel, half, step):
        bit = halved_bit(half, step)
        source, pairs = own_part(channel, half, step)
        return pltpu.make_async_remote_copy(
            src_ref=source.at[:, 1 - ((worker >> bit) & 1), :, pairs],
            dst_ref=received[half][step].at[channel],
            send_sem=send_sem.at[channel, half, step],
            recv_sem=recv_sem.at[channel, half, step],
            device_id=(partner(bit), tile),
            device_id_type=MESH,
        )

    def step_sum(channel, half, step):
        mine = (worker >> halved_bit(half, step)) & 1
        source, pairs = own_part(channel, half, step)
        arrived = received[half][step].at[channel]
        target = kept[half][step].at[channel]
        if step == bits - 1:
            target[...] = source[0, mine, 0, pairs] + arrived[0, 0]
            return
        low, low_next = arrived.shape[1], target.shape[2]
        for a in range(arrived.shape[0]):
            for b in range(low):
                at = a * low + b
                target[at // (2 * low_next), at // low_next % 2, at % low_next] = source[a, mine, b, pairs] + arrived[a, b]

    copies = {}

    def advance(channel, step):
        for half in range(2):
            copies[channel, half].wait()
            step_sum(channel, half, step)
            if step < bits - 1:
                copies[channel, half] = step_copy(channel, half, step + 1)
                copies[channel, half].start()

    width = 4 * SUB
    columns, rows = columns_ref[...], rows_ref[...]
    lane = lax.broadcasted_iota(jnp.int32, (1, SUBW * SUB), 1)
    row_at = lane % SUB
    for s in range(SUBW):
        row_at = row_at + jnp.where(lane // SUB == s, corners_ref[0, worker * SUBW + s], 0)
    stripe = lax.broadcasted_iota(jnp.int32, (width, GCW), 0)
    across = lax.broadcasted_iota(jnp.int32, (width, GCW), 1) - stripe % SUB
    group = lax.broadcasted_iota(jnp.int32, (width, width), 0) // SUB
    same = group == lax.broadcasted_iota(jnp.int32, (width, width), 1) // SUB

    low_lanes = lax.broadcasted_iota(jnp.int32, (SUB, width), 1) < 2 * SUB

    def transform(channel):
        pictures = jnp.concatenate(
            [kept[half][bits - 1][channel].reshape(HALF * SUBW, width) for half in range(2)], axis=0
        )
        first = jnp.dot(pictures, columns, precision=highest, preferred_element_type=jnp.float32)
        first_ref[0] = first[:, :width]
        first_ref[1] = first[:, width:]
        plain, turned = [], []
        for j in range(SUBW // 2):
            even, odd = [
                jnp.concatenate(
                    [first_ref[side, pl.ds(2 * j + s, FOLD, stride=SUBW), :] for side in range(2)], axis=0
                )
                for s in range(2)
            ]
            plain.append(jnp.where(low_lanes, even, pltpu.roll(odd, 2 * SUB, 1)))
            turned.append(jnp.where(low_lanes, pltpu.roll(even, 2 * SUB, 1), odd))
        stacked = jnp.concatenate([jnp.concatenate(plain, axis=1), jnp.concatenate(turned, axis=1)], axis=0)
        spectra = jnp.dot(rows, stacked, precision=highest, preferred_element_type=jnp.float32)
        for j in range(SUBW // 2):
            spectrum = spectra[:, j * width:(j + 1) * width]
            spread = jnp.where(same, jnp.concatenate([spectrum] * 4, axis=0), 0.0)
            high, low = split(spread)
            column = [corners_ref[1, worker * SUBW + 2 * j + side] - worker * GCW for side in range(2)]
            target = across == jnp.where(stripe < 2 * SUB, column[0], column[1])
            target = jnp.where(target, 1.0, 0.0).astype(jnp.bfloat16)
            wide = jnp.dot(jnp.concatenate([high, low], axis=0), target, preferred_element_type=jnp.float32)
            high, low = split(wide[:width] + wide[width:])
            for side in range(2):
                for part in range(2):
                    here = slice((2 * side + part) * SUB, (2 * side + part + 1) * SUB)
                    there = slice((2 * j + side) * SUB, (2 * j + side + 1) * SUB)
                    placed[2 * channel + part, there, :GCW] = high[here]
                    placed[2 * channel + part, there, GCW:] = low[here]

    def tile_rows(channel, which, store):
        line = lax.broadcasted_iota(jnp.int32, (height, SUBW * SUB), 0) + which * height
        select = jnp.where(line == row_at, 1.0, 0.0).astype(jnp.bfloat16)
        for part in range(2):
            both = jnp.dot(select, placed[2 * channel + part], preferred_element_type=jnp.float32)
            store[part] = both[:, :GCW] + both[:, GCW:]

    blocks = waves_ref.shape[0]
    steps = blocks // UNROLL
    offset = (lax.broadcasted_iota(jnp.int32, (SUB, ROWS), 0) - SUB // 2).astype(jnp.float32) * (1.0 / SUB)
    square = offset * offset
    low_half = lax.broadcasted_iota(jnp.int32, (FOLD, width), 1) < 2 * SUB

    def picture(channel, block):
        factor = scale_ref[channel]
        first, second, third = [coords_ref[axis, pl.ds(block, 1), :] * factor for axis in range(3)]
        waves = waves_ref[block]
        depth = third * square
        sine, cosine = sincos_turns(first * offset + depth)
        real, imag = waves[2 * channel:2 * channel + 1, :], waves[2 * channel + 1:2 * channel + 2, :]
        left_high, left_low = split(
            jnp.concatenate([real * cosine - imag * sine, real * sine + imag * cosine], axis=1)
        )
        sine, cosine = sincos_turns(second * offset + depth)
        sine_high, sine_low = split(sine)
        cosine_high, cosine_low = split(cosine)
        right = jnp.concatenate(
            [
                jnp.concatenate([cosine_high, -sine_high], axis=1),
                jnp.concatenate([sine_high, cosine_high], axis=1),
                jnp.concatenate([cosine_low, -sine_low], axis=1),
                jnp.concatenate([sine_low, cosine_low], axis=1),
            ],
            axis=0,
        )
        product = dot_nt(jnp.concatenate([left_high, left_low], axis=0), right)
        product = product[:SUB] + product[SUB:]
        upper, lower = product[:FOLD], product[FOLD:]
        return jnp.where(low_half, upper, lower) + pltpu.roll(jnp.where(low_half, lower, upper), 2 * SUB, 1)

    def fill(channel, begin, end):
        def body(step, carry):
            base = step * UNROLL
            group = [picture(channel, base + k) for k in range(UNROLL)]
            for k in range(UNROLL):
                pictures_ref[pl.ds(base + k, FOLD, stride=blocks), :] = group[k]
            return carry

        lax.fori_loop(begin, end, body, 0)

    def merge(channel):
        subgrids = SUBW * workers
        named = lax.broadcasted_iota(jnp.int32, (subgrids, blocks), 0) == labels_ref[...]
        alive = lax.broadcasted_iota(jnp.int32, (subgrids, blocks), 1) < live_ref[0]
        choose = jnp.where(named & alive, 1.0, 0.0).astype(jnp.bfloat16)
        for half in range(2):
            for x in range(half * HALF, (half + 1) * HALF):
                high, low = split(pictures_ref[x * blocks:(x + 1) * blocks])
                both = jnp.dot(choose, jnp.concatenate([high, low], axis=1), preferred_element_type=jnp.float32)
                both = both[:, :width] + both[:, width:]
                for w in range(workers):
                    data_ref[channel, w // 2, w % 2, 0, x] = both[w * SUBW:(w + 1) * SUBW]
            if channel == 0 and half == 0:
                pl.semaphore_wait(barrier, bits + tiles - 1)
            copies[channel, half] = step_copy(channel, half, 0)
            copies[channel, half].start()

    sent = []

    def spread_tiles(channel):
        for far in range(tiles - 1, 0, -1):
            which = lax.rem(tile + far, tiles)
            tile_rows(channel, which, outgoing.at[channel, far - 1])
            copy = pltpu.make_async_remote_copy(
                src_ref=outgoing.at[channel, far - 1],
                dst_ref=incoming.at[channel, far - 1],
                send_sem=tile_send.at[channel, far - 1],
                recv_sem=tile_recv.at[channel, far - 1],
                device_id=(worker, which),
                device_id_type=MESH,
            )
            copy.start()
            sent.append(copy)
        tile_rows(channel, tile, out_ref.at[pl.ds(2 * channel, 2)])

    fill(0, 0, steps)
    merge(0)
    done = 0
    for step in range(bits):
        until = steps - (4 * steps // 5 >> step)
        fill(1, done, until)
        done = until
        advance(0, step)
    transform(0)
    spread_tiles(0)
    fill(1, done, steps)
    merge(1)
    for step in range(bits):
        advance(1, step)
    transform(1)
    spread_tiles(1)
    for copy in sent:
        copy.wait()
    for channel in range(CH):
        total = out_ref[2 * channel:2 * channel + 2]
        for far in range(tiles - 1):
            total = total + incoming[channel, far]
        out_ref[2 * channel:2 * channel + 2] = total


def gridded(coords, waves, labels, live, corners, scale, workers, tiles, height):
    bits = workers.bit_length() - 1
    blocks = waves.shape[0]
    width = 4 * SUB
    received, kept = [], []
    tail = (HALF, SUBW, width)
    for order in stage_shapes(workers):
        for step in range(bits):
            count = workers >> step
            low = 1 << order[step]
            received.append(pltpu.VMEM((CH, count // (2 * low), low) + tail, jnp.float32))
            if step < bits - 1:
                low = 1 << order[step + 1]
                kept.append(pltpu.VMEM((CH, count // 2 // (2 * low), 2, low) + tail, jnp.float32))
            else:
                kept.append(pltpu.VMEM((CH,) + tail, jnp.float32))
    columns, rows = transform_matrices()
    vmem = pl.BlockSpec(memory_space=pltpu.VMEM)
    smem = pl.BlockSpec(memory_space=pltpu.SMEM)
    return pl.pallas_call(
        functools.partial(grid_kernel, workers, tiles),
        out_shape=jax.ShapeDtypeStruct((2 * CH, height, GCW), jnp.float32),
        in_specs=[smem, smem, smem, vmem, vmem, vmem, vmem, vmem],
        out_specs=vmem,
        scratch_shapes=received + kept + [
            pltpu.VMEM((FOLD * blocks, width), jnp.float32),
            pltpu.VMEM((CH, workers // 2, 2, 1, FOLD, SUBW, width), jnp.float32),
            pltpu.VMEM((2, FOLD * SUBW, width), jnp.float32),
            pltpu.VMEM((2 * CH, SUBW * SUB, 2 * GCW), jnp.bfloat16),
            pltpu.VMEM((CH, tiles - 1, 2, height, GCW), jnp.float32),
            pltpu.VMEM((CH, tiles - 1, 2, height, GCW), jnp.float32),
            pltpu.SemaphoreType.DMA((CH, 2, bits)),
            pltpu.SemaphoreType.DMA((CH, 2, bits)),
            pltpu.SemaphoreType.DMA((CH, tiles - 1)),
            pltpu.SemaphoreType.DMA((CH, tiles - 1)),
        ],
        compiler_params=pltpu.CompilerParams(
            collective_id=0, has_side_effects=True, vmem_limit_bytes=56 * 1024 * 1024
        ),
        name="grid_blocks",
    )(live, scale, jnp.transpose(corners), labels.reshape(1, blocks), coords, waves, jnp.asarray(columns), jnp.asarray(rows))


def local(height, block_coords, block_visibilities, subgrid_of_block, live_blocks, corners, channel_scale):
    workers = lax.axis_size("work")
    tiles = lax.axis_size("tile")
    return gridded(
        jnp.transpose(block_coords, (1, 0, 2)), block_visibilities, subgrid_of_block, live_blocks, corners,
        channel_scale, workers, tiles, height,
    )


def solution(mesh):
    height = 64
    return jax.shard_map(
        functools.partial(local, height),
        mesh=mesh,
        in_specs=(
            P(("work", "tile"), None, None),
            P(("work", "tile"), None, None),
            P(("work", "tile")),
            P(("work", "tile")),
            P(),
            P(),
        ),
        out_specs=P(None, "tile", "work"),
        check_vma=False,
    )
```
